32 devices in a mesh: rep: 8 (over z, y), grp: 4 (over x, core).
Axes of the slice: x: 2, y: 2, z: 4, core: 2. Of those that a mesh axis runs over, the one named last changes fastest.
Arguments:
- tokens: bfloat16 [32768, 1024], P(('rep', 'grp')), may hold values from -6 to 6
- segments: int32 [32768], P(('rep', 'grp')), may hold values from 0 to 79, never falling along the last dimension, each value on 1 to 800 neighbouring positions
- attn_gain: bfloat16 [1024], P('grp'), may hold values from 0.3984375 to 1.59375
- w_query: bfloat16 [1024, 1024], P('grp'), may hold values from -0.1875 to 0.1875
- w_key: bfloat16 [1024, 512], P('grp'), may hold values from -0.1875 to 0.1875
- w_value: bfloat16 [1024, 512], P('grp'), may hold values from -0.1875 to 0.1875
- query_gain: bfloat16 [64], P('grp'), may hold values from 0.099609375 to 1.8984375
- key_gain: bfloat16 [64], P('grp'), may hold values from 0.099609375 to 1.8984375
- w_out: bfloat16 [1024, 1024], P('grp'), may hold values from -0.75 to 0.75
- ffn_gain: bfloat16 [1024], P('grp'), may hold values from 0.3984375 to 1.59375
- w_gate: bfloat16 [1024, 4608], P('grp'), may hold values from -0.1875 to 0.1875
- w_up: bfloat16 [1024, 4608], P('grp'), may hold values from -0.1875 to 0.1875
- w_down: bfloat16 [4608, 1024], P('grp'), may hold values from -0.09375 to 0.09375
- out_grad: bfloat16 [32768, 1024], P(('rep', 'grp')), may hold values from -6 to 6
Outputs:
- outputs: bfloat16 [32768, 1024], P(('rep', 'grp'))
- input_grad: bfloat16 [32768, 1024], P(('rep', 'grp'))
- attn_gain_grad: float32 [1024], P('grp')
- query_wgrad: float32 [1024, 1024], P('grp')
- key_wgrad: float32 [1024, 512], P('grp')
- value_wgrad: float32 [1024, 512], P('grp')
- query_gain_grad: float32 [64], P('grp')
- key_gain_grad: float32 [64], P('grp')
- out_wgrad: float32 [1024, 1024], P('grp')
- ffn_gain_grad: float32 [1024], P('grp')
- gate_wgrad: float32 [1024, 4608], P('grp')
- up_wgrad: float32 [1024, 4608], P('grp')
- down_wgrad: float32 [4608, 1024], P('grp')
The draws below stay inside these ranges and needn't reach their ends.
Inputs may be any that keep to these rules, and one draw needn't show every extreme that they name: `segments`: document numbers never fall along the tokens; each document has 1 to 800 tokens, and some document has exactly 800.
All inputs are finite; a program needn't handle non-finite values.
Results may differ from the reference program's by a relative error of at most 0.017.
Values may be sent and summed in bfloat16 or wider, within the bound.
No kernel may reach another device: no remote copies, remote signals or barrier semaphores. Data moves between devices by JAX's collectives and lax.ppermute only.
A program may use at most 320 MiB of HBM per device.

```python
import math
from functools import partial
import jax
import jax.numpy as jnp
import numpy as np
from jax import lax

D = 1024
H = 16
KV = 8
HD = 64
FF = 4608
SEQ = 1024
TOKENS = 32768
DOCS = 80
DOC_MOST = 800


def steps_of(key, dims, shards, least, largest):
    level, own = 1.0, jax.random.fold_in(key, 6)
    for dim, blocks in shards:
        heights = jnp.exp(jax.random.uniform(jax.random.fold_in(own, dim), (blocks,), jnp.float32, least / len(shards), largest / len(shards)))
        level = level * jnp.repeat(heights, dims[dim] // blocks).reshape([-1 if axis == dim else 1 for axis in range(len(dims))])
    return level


def length_profile(amount, total, bound, slope):
    portions = [(1 << 20) // math.isqrt(rank ** slope) + 1 for rank in range(2, amount + 1)]
    rest, holding = total - bound - (amount - 1), [1] * (amount - 1)
    while rest > 0:
        candidates = [i for i in range(amount - 1) if holding[i] < bound]
        pool, left = sum([portions[i] for i in candidates]), rest
        for i in candidates:
            addition = min(bound - holding[i], max(1, left * portions[i] // pool), rest)
            holding[i] = holding[i] + addition
            rest = rest - addition
    return np.array([bound] + holding)


def ragged(rng, number_of, total, reach, lean):
    if number_of == 2:
        one = jax.random.randint(rng, (), max(1, total - reach), min(reach, total - 1) + 1)
        return jnp.stack([one, total - one])
    tallies = jnp.asarray(length_profile(number_of, total, reach, lean), jnp.int32)
    twos = (number_of - 1) // 2
    giver, taker = tallies[1:1 + 2 * twos:2], tallies[2:2 + 2 * twos:2]
    slack = jnp.minimum(giver - 1, reach - taker)
    moved = jax.random.randint(jax.random.fold_in(rng, 1), (twos,), 0, 1 << 20) % (slack + 1)
    tallies = tallies.at[1:1 + 2 * twos:2].set(giver - moved).at[2:2 + 2 * twos:2].set(taker + moved)
    return tallies[jax.random.permutation(jax.random.fold_in(rng, 2), number_of)]


def noise(own_key, dims, scale, bound, pieces=(), held_as=jnp.bfloat16):
    entries = scale * jax.random.normal(own_key, dims, jnp.float32)
    if pieces:
        entries = entries * steps_of(own_key, dims, pieces, -0.22, 0.18)
    return jnp.clip(entries, -bound, bound).astype(held_as)


def setup_inputs(seed: int = 0) -> dict:
    key_list = jax.random.split(jax.random.key(seed), 15)
    return {
        "tokens": noise(key_list[0], (TOKENS, D), 1.0, 6.0, ((0, 32),)),
        "segments": jnp.searchsorted(jnp.cumsum(ragged(key_list[1], DOCS, TOKENS, DOC_MOST, 1)), jnp.arange(TOKENS), side="right").astype(jnp.int32),
        "attn_gain": jnp.clip(1.0 + 0.12 * jax.random.normal(key_list[2], (D,), jnp.float32), 0.3984375, 1.59375).astype(jnp.bfloat16),
        "w_query": noise(key_list[3], (D, H * HD), D ** -0.5, 0.1875, ((0, 4),)),
        "w_key": noise(key_list[4], (D, KV * HD), D ** -0.5, 0.1875, ((0, 4),)),
        "w_value": noise(key_list[5], (D, KV * HD), D ** -0.5, 0.1875, ((0, 4),)),
        "query_gain": jnp.clip(1.0 + 0.18 * jax.random.normal(key_list[6], (HD,), jnp.float32), 0.099609375, 1.8984375).astype(jnp.bfloat16),
        "key_gain": jnp.clip(1.0 + 0.18 * jax.random.normal(key_list[7], (HD,), jnp.float32), 0.099609375, 1.8984375).astype(jnp.bfloat16),
        "w_out": noise(key_list[8], (H * HD, D), (H * HD // 16) ** -0.5, 0.75, ((0, 4),)),
        "ffn_gain": jnp.clip(1.0 + 0.12 * jax.random.normal(key_list[9], (D,), jnp.float32), 0.3984375, 1.59375).astype(jnp.bfloat16),
        "w_gate": noise(key_list[10], (D, FF), D ** -0.5, 0.1875, ((0, 4),)),
        "w_up": noise(key_list[11], (D, FF), D ** -0.5, 0.1875, ((0, 4),)),
        "w_down": noise(key_list[12], (FF, D), FF ** -0.5, 0.09375, ((0, 4),)),
        "out_grad": noise(key_list[13], (TOKENS, D), 1.0, 6.0, ((0, 32),)),
    }


epsilon = 1e-05
theta_base = 1000000.0

@jax.custom_vjp
def low(v):
    return lax.optimization_barrier(v.astype(jnp.bfloat16)).astype(jnp.float32)

@jax.custom_vjp
def low_back(v):
    return v

def low_keep(v):
    return (low(v), None)

def low_pass(kept, grad):
    return (grad,)

def back_keep(v):
    return (v, None)

def back_low(kept, grad):
    return (low(grad),)
low.defvjp(low_keep, low_pass)
low_back.defvjp(back_keep, back_low)

def matmul_high(left, right):
    return jnp.dot(left, right, precision=lax.Precision.HIGHEST, preferred_element_type=jnp.float32)

def rms_norm(values):
    return values * lax.rsqrt(lax.optimization_barrier(jnp.mean(values * values, axis=-1, keepdims=True)) + epsilon)

def doc_positions(segment_rows):
    seq_len = segment_rows.shape[-1]
    places = jnp.arange(seq_len, dtype=jnp.int32)
    keep_mask = (segment_rows[:, :, None] == segment_rows[:, None, :]) & (places[None, None, :] <= places[None, :, None])
    return (lax.optimization_barrier(jnp.sum(keep_mask.astype(jnp.int32), axis=-1)) - 1).astype(jnp.float32)

def rope_tables(positions):
    half_width = HD // 2
    freqs = theta_base ** (-(2.0 * jnp.arange(half_width, dtype=jnp.float32)) / HD)
    angles = positions[:, None] * freqs[None, :]
    return (jnp.cos(angles), jnp.sin(angles))

def rotate(values, cos_table, sin_table):
    half_width = values.shape[-1] // 2
    first_half = values[..., :half_width]
    second_half = values[..., half_width:]
    cos_rows = cos_table[:, None, :]
    sin_rows = sin_table[:, None, :]
    return jnp.concatenate([first_half * cos_rows - second_half * sin_rows, second_half * cos_rows + first_half * sin_rows], axis=-1)

def attend_reference(items):
    query, keys, values, segment = items
    places = jnp.arange(SEQ, dtype=jnp.int32)
    keep_mask = (segment[:, None] == segment[None, :]) & (places[None, :] <= places[:, None])
    raw = jnp.einsum('qcrd,kcd->crqk', query, keys, precision=lax.Precision.HIGHEST) * HD ** (-0.5)
    scores = jnp.where(keep_mask[None, None], low_back(raw), -1e+30)
    row_max = lax.optimization_barrier(jnp.max(scores, axis=-1, keepdims=True))
    exp_scores = jnp.exp(scores - row_max)
    probs = exp_scores / lax.optimization_barrier(jnp.sum(exp_scores, axis=-1, keepdims=True))
    return jnp.einsum('crqk,kcd->qcrd', low(probs), values, precision=lax.Precision.HIGHEST)

def layer_forward(inputs, attn_gain, w_query, w_key, w_value, query_gain, key_gain, w_out, ffn_gain, w_gate, w_up, w_down, segment_rows):
    token_count = inputs.shape[0]
    seq_count = token_count // SEQ
    group_heads = H // KV
    positions = doc_positions(segment_rows).reshape(token_count)
    cos_table, sin_table = rope_tables(positions)
    first_low = low(rms_norm(inputs) * attn_gain)
    query_proj = low_back(matmul_high(first_low, w_query)).reshape(token_count, H, HD)
    key_proj = low_back(matmul_high(first_low, w_key)).reshape(token_count, KV, HD)
    value_low = low(low_back(matmul_high(first_low, w_value)))
    query_low = low(rotate(rms_norm(query_proj) * query_gain, cos_table, sin_table))
    key_low = low(rotate(rms_norm(key_proj) * key_gain, cos_table, sin_table))
    mixed = lax.map(jax.checkpoint(attend_reference), (query_low.reshape(seq_count, SEQ, KV, group_heads, HD), key_low.reshape(seq_count, SEQ, KV, HD), value_low.reshape(seq_count, SEQ, KV, HD), segment_rows))
    mixed_low = low(low_back(mixed.reshape(token_count, H * HD)))
    residual = inputs + low_back(matmul_high(mixed_low, w_out))
    second_low = low(rms_norm(residual) * ffn_gain)
    gate_val = low_back(matmul_high(second_low, w_gate))
    up_val = low_back(matmul_high(second_low, w_up))
    inner_low = low(jax.nn.silu(gate_val) * up_val)
    return residual + matmul_high(inner_low, w_down)

def reference(tokens, segments, attn_gain, w_query, w_key, w_value, query_gain, key_gain, w_out, ffn_gain, w_gate, w_up, w_down, out_grad):
    seq_total = TOKENS // SEQ
    per_step = math.gcd(seq_total, max(1, 4096 // SEQ))
    step_count = seq_total // per_step
    params = (attn_gain.astype(jnp.float32), w_query.astype(jnp.float32), w_key.astype(jnp.float32), w_value.astype(jnp.float32), query_gain.astype(jnp.float32), key_gain.astype(jnp.float32), w_out.astype(jnp.float32), ffn_gain.astype(jnp.float32), w_gate.astype(jnp.float32), w_up.astype(jnp.float32), w_down.astype(jnp.float32))
    token_steps = tokens.astype(jnp.float32).reshape(step_count, per_step * SEQ, D)
    seg_steps = segments.reshape(step_count, per_step, SEQ)
    grad_steps = out_grad.astype(jnp.float32).reshape(step_count, per_step * SEQ, D)

    def one_step(totals, items):
        step_tokens, step_segs, step_grad = items
        outputs_step, pull = jax.vjp(partial(layer_forward, segment_rows=step_segs), step_tokens, *params)
        grads = pull(step_grad)
        new_totals = tuple((total + grad for total, grad in zip(totals, grads[1:])))
        return (new_totals, (outputs_step.astype(jnp.bfloat16), grads[0].astype(jnp.bfloat16)))
    zeros_init = tuple((jnp.zeros_like(param) for param in params))
    totals, (outputs_all, input_all) = lax.scan(one_step, zeros_init, (token_steps, seg_steps, grad_steps))
    return (outputs_all.reshape(TOKENS, D), input_all.reshape(TOKENS, D), totals[0], totals[1], totals[2], totals[3], totals[4], totals[5], totals[6], totals[7], totals[8], totals[9], totals[10])
```

```python
import jax
import jax.numpy as jnp
from jax import lax
from jax.experimental import pallas as pl
from jax.experimental.pallas import tpu as pltpu
from jax.sharding import PartitionSpec as P

D = 1024
H = 16
KV = 8
HD = 64
FF = 4608
SEQ = 1024
GRP = 4
CHUNKS = 3
TILE = FF // GRP // CHUNKS
ROWS = D // GRP
PAIR = 2 * TILE
GROUP_Q = H // GRP * HD
GROUP_K = KV // GRP * HD
GROUP_QK = GROUP_Q + GROUP_K
GROUP_ALL = GROUP_QK + GROUP_K
BLOCK = 256

epsilon = 1e-05
theta_base = 1000000.0
score_scale = HD ** (-0.5)
log2_e = 1.4426950408889634
ln_2 = 0.6931471805599453

f32 = jnp.float32
bf16 = jnp.bfloat16


def dot_nn(left, right):
    return lax.dot_general(left, right, (((1,), (0,)), ((), ())), preferred_element_type=f32)


def dot_nt(left, right):
    return lax.dot_general(left, right, (((1,), (1,)), ((), ())), preferred_element_type=f32)


def dot_tn(left, right):
    return lax.dot_general(left, right, (((0,), (0,)), ((), ())), preferred_element_type=f32)


def rms_scale(values):
    return lax.rsqrt(jnp.mean(values * values, axis=-1, keepdims=True) + epsilon)


def norm_back(grad_unit, unit, inverse):
    return inverse * (grad_unit - unit * jnp.mean(grad_unit * unit, axis=-1, keepdims=True))


def block_of(ref, block, rows):
    return ref.at[pl.ds(pl.multiple_of(block * rows, rows), rows)]


def tie(*values):
    return lax.optimization_barrier(values)


def split_two(values):
    high = values.astype(bf16)
    return high, (values - high.astype(f32)).astype(bf16)


def head_mean(values, spread):
    high, rest = split_two(values)
    return dot_nn(high, spread) + dot_nn(rest, spread)


def swap_halves(values):
    width = values.shape[-1]
    lane = lax.broadcasted_iota(jnp.int32, values.shape, 1)
    ahead = pltpu.roll(values, width - 32, 1)
    behind = pltpu.roll(values, 32, 1)
    return jnp.where((lane & 63) < 32, ahead, behind)


def three_lanes(values):
    high = values.astype(bf16).astype(f32)
    rest = values - high
    mid = rest.astype(bf16).astype(f32)
    lane = lax.broadcasted_iota(jnp.int32, values.shape, 1)
    out = jnp.where(lane == 0, high, jnp.where(lane == 1, mid, jnp.where(lane == 2, rest - mid, 0.0)))
    return out.astype(bf16)


def three_ones(rows):
    lane = lax.broadcasted_iota(jnp.int32, (rows, HD), 1)
    return jnp.where(lane < 3, 1.0, 0.0).astype(bf16)


def fill_mask(mask, seg_col, seg_row):
    count = mask.shape[0]
    for start in range(0, count, BLOCK):
        rows = lax.broadcasted_iota(jnp.int32, (BLOCK, count), 0) + start
        cols = lax.broadcasted_iota(jnp.int32, (BLOCK, count), 1)
        keep = (seg_col[start : start + BLOCK, :] == seg_row[...]) & (cols <= rows)
        mask[start : start + BLOCK, :] = jnp.where(keep, 1.0, 0.0)


def place_rows(place_ref, held, pieces, start=0, stop=None):
    own, core, far, far_core = pieces
    g, low = place_ref[0], place_ref[1]
    rows = held.shape[0] // GRP
    quarter = rows // 4
    block_of(held, g, rows)[...] = own
    block_of(held, g ^ 1, rows)[...] = core
    for q, piece in ((2, far), (3, far_core)):
        for k in range(4):
            block_of(held, (g ^ q) * 4 + (low ^ k), quarter)[...] = piece[k]


def pack_kernel(place_ref, w_query, w_key, w_value, w_out, out, quarter):
    for a in range(GRP):
        start = a * GROUP_ALL
        out[:, start : start + GROUP_Q] = w_query[:, a * GROUP_Q : (a + 1) * GROUP_Q]
        out[:, start + GROUP_Q : start + GROUP_QK] = w_key[:, a * GROUP_K : (a + 1) * GROUP_K]
        out[:, start + GROUP_QK : start + GROUP_ALL] = w_value[:, a * GROUP_K : (a + 1) * GROUP_K]
    out[:, GRP * GROUP_ALL :] = w_out[...]
    quarter[...] = block_of(out, place_ref[1], ROWS // 4)[...]


def quarters_kernel(place_ref, gate, up, down, *outs):
    part = ROWS // 4
    for i, out in enumerate(outs):
        for k, weight in ((0, gate), (1, up)):
            for a in range(GRP):
                first = (a * CHUNKS + i) * TILE
                start = (k * GRP + a) * part
                out[start : start + part, :] = weight[:, first : first + TILE]
        out[2 * GRP * part :, :] = down[i * TILE : (i + 1) * TILE, :].T


def first_kernel(tokens, grad, gain, first, first_t, grad_t):
    inputs = tokens[...].astype(f32)
    low = (inputs * rms_scale(inputs) * gain[...]).astype(bf16)
    first[...] = low
    first_t[...] = low.T
    grad_t[...] = grad[...].T


def attend_kernel(
    place_ref, first, own, core, far, far_core, cos, sin, gain, seg_col, seg_row, spread,
    proj, qk_low, v_low, mixed, lse, weights, mask, ones_v,
):
    count = first.shape[0]
    place_rows(place_ref, weights, (own[...], core[...], far, far_core))

    @pl.when(pl.program_id(0) == 0)
    def _():
        fill_mask(mask, seg_col, seg_row)

    @pl.loop(0, count // BLOCK)
    def _(block):
        rows = pl.ds(pl.multiple_of(block * BLOCK, BLOCK), BLOCK)
        values = dot_nn(first[rows, :], weights[...])
        qk = values[:, :GROUP_QK]
        proj[rows, :] = qk
        inverse = lax.rsqrt(head_mean(qk * qk, spread[...]) + epsilon)
        normed = qk * inverse * gain[...]
        cos_rows = jnp.concatenate([cos[rows, :]] * (GROUP_QK // 128), axis=1)
        sin_rows = jnp.concatenate([sin[rows, :]] * (GROUP_QK // 128), axis=1)
        qk_low[rows, :] = (normed * cos_rows + swap_halves(normed) * sin_rows).astype(bf16)
        v_low[rows, :] = values[:, GROUP_QK:].astype(bf16)

    for j in range(GROUP_K // HD):
        ones_v[:, :HD] = v_low[:, j * HD : (j + 1) * HD]
        ones_v[:, HD:] = jnp.ones((count, HD), bf16)
        keys = qk_low[:, GROUP_Q + j * HD : GROUP_Q + (j + 1) * HD]
        for start in range(0, count, BLOCK):
            stop = start + BLOCK
            pair = jnp.concatenate(
                [
                    qk_low[start:stop, (2 * j + i) * HD : (2 * j + i + 1) * HD]
                    for i in range(2)
                ],
                axis=0,
            )
            scores = dot_nt(pair, keys[:stop])
            keep = mask[start:stop, :stop]
            weights_low = (jnp.exp2(scores) * jnp.concatenate([keep, keep], axis=0)).astype(bf16)
            summed = dot_nn(weights_low, ones_v[:stop, :])
            total = summed[:, HD:]
            part = (summed[:, :HD] / total).astype(bf16)
            log_total = jnp.log2(total)
            for i in range(2):
                lanes = slice((2 * j + i) * HD, (2 * j + i + 1) * HD)
                mixed[start:stop, lanes] = part[i * BLOCK : (i + 1) * BLOCK]
                lse[start:stop, lanes] = log_total[i * BLOCK : (i + 1) * BLOCK]


def attend_back_kernel(
    place_ref, residual_low, w_out, weights, first_t, proj, qk_low, v_low, mixed, lse, cos, sin, gain,
    seg_col, seg_row, spread,
    first_low, kept, sent, gain_grad,
    mask, mixed_grad, delta, grads, key_grad, value_grad, low_grads, key_ext, value_ext, first_grad,
):
    count = residual_low.shape[0]
    step = pl.program_id(0)

    @pl.when(step == 0)
    def _():
        fill_mask(mask, seg_col, seg_row)
        first_grad[...] = jnp.zeros_like(first_grad)
        gain_grad[...] = jnp.zeros_like(gain_grad)

    @pl.loop(0, count // BLOCK)
    def _(block):
        rows = pl.ds(pl.multiple_of(block * BLOCK, BLOCK), BLOCK)
        low = dot_nt(residual_low[rows, :], w_out[...]).astype(bf16)
        mixed_grad[rows, :] = low
        product = low.astype(f32) * mixed[rows, :].astype(f32)
        delta[rows, :] = head_mean(product, spread[:GROUP_Q, :GROUP_Q]) * HD

    for j in range(GROUP_K // HD):
        key_ext[:, :HD] = qk_low[:, GROUP_Q + j * HD : GROUP_Q + (j + 1) * HD]
        key_ext[:, HD:] = three_ones(count)
        value_ext[:, :HD] = v_low[:, j * HD : (j + 1) * HD]
        value_ext[:, HD:] = three_ones(count)
        key_grad[...] = jnp.zeros_like(key_grad)
        value_grad[...] = jnp.zeros_like(value_grad)
        for start in range(0, count, BLOCK):
            stop = start + BLOCK
            query_rows, grad_rows = [], []
            for i in range(2):
                lanes = slice((2 * j + i) * HD, (2 * j + i + 1) * HD)
                query_rows.append(
                    jnp.concatenate(
                        [qk_low[start:stop, lanes], three_lanes(-lse[start:stop, lanes])], axis=1
                    )
                )
                grad_rows.append(
                    jnp.concatenate(
                        [mixed_grad[start:stop, lanes], three_lanes(-delta[start:stop, lanes])],
                        axis=1,
                    )
                )
            query_ext = jnp.concatenate(query_rows, axis=0)
            grad_ext = jnp.concatenate(grad_rows, axis=0)
            keep = mask[start:stop, :stop]
            probs = jnp.exp2(dot_nt(query_ext, key_ext[:stop, :])) * jnp.concatenate(
                [keep, keep], axis=0
            )
            score_grad = (probs * dot_nt(grad_ext, value_ext[:stop, :])).astype(bf16)
            query_grad = dot_nn(score_grad, key_ext[:stop, :]) * score_scale
            for i in range(2):
                lanes = slice((2 * j + i) * HD, (2 * j + i + 1) * HD)
                grads[start:stop, lanes] = query_grad[i * BLOCK : (i + 1) * BLOCK, :HD]
            key_grad[:stop, :] += dot_tn(score_grad, query_ext)
            value_grad[:stop, :] += dot_tn(probs.astype(bf16), grad_ext)
        grads[:, GROUP_Q + j * HD : GROUP_Q + (j + 1) * HD] = key_grad[:, :HD] * ln_2
        low_grads[:, GROUP_QK + j * HD : GROUP_QK + (j + 1) * HD] = value_grad[:, :HD].astype(bf16)

    @pl.loop(0, count // BLOCK)
    def _(block):
        rows = pl.ds(pl.multiple_of(block * BLOCK, BLOCK), BLOCK)
        cos_rows = jnp.concatenate([cos[rows, :]] * (GROUP_QK // 128), axis=1)
        sin_rows = jnp.concatenate([sin[rows, :]] * (GROUP_QK // 128), axis=1)
        turned = grads[rows, :]
        turned = turned * cos_rows - swap_halves(turned) * sin_rows
        qk = proj[rows, :]
        inverse = lax.rsqrt(head_mean(qk * qk, spread[...]) + epsilon)
        unit = qk * inverse
        gain_grad[...] += jnp.sum(turned * unit, axis=0, keepdims=True)
        scaled = turned * gain[...]
        back = inverse * (scaled - unit * head_mean(scaled * unit, spread[...]))
        low_grads[rows, :GROUP_QK] = back.astype(bf16)
        first_grad[rows, :] += dot_nt(low_grads[rows, :], weights[...])

    for x in range(2):
        for c in range(2):
            rows = pl.ds(pl.multiple_of((place_ref[0] ^ (2 * x + c)) * ROWS, ROWS), ROWS)
            part = dot_nn(first_t[rows, :], low_grads[...]).astype(bf16)
            if c == 0:
                kept[x] = part
            else:
                sent[x] = part

    @pl.when(step == pl.num_programs(0) - 1)
    def _():
        first_low[...] = first_grad[...].astype(bf16)


def middle_kernel(
    place_ref, mixed0, mixed1, tokens, gain, own, core, far, far_core, residual, second, second_t, w_out
):
    @pl.when(pl.program_id(0) == 0)
    def _():
        place_rows(place_ref, w_out, (own[...], core[...], far, far_core))

    mixed = jnp.concatenate([mixed0[...], mixed1[...]], axis=1)
    total = tokens[...].astype(f32) + dot_nn(mixed, w_out[...])
    residual[...] = total
    low = (total * rms_scale(total) * gain[...]).astype(bf16)
    second[...] = low
    second_t[...] = low.T


def ffn_kernel(
    place_ref, second, second_t, grad, grad_t,
    gate0, gate1, up0, up1, core_gate0, core_gate1, core_up0, core_up1, far, far_core,
    down, core_down,
    out, second_grad, gu_kept, gu_sent, dn_kept, dn_sent,
    w_both, w_down, inner_low, both_low, out_sum, grad_sum,
):
    step = pl.program_id(0)
    g, low = place_ref[0], place_ref[1]
    odd = (g & 1) == 1
    count = second.shape[0]
    block_rows = min(512, count)
    quarter = ROWS // 4
    for j, (gate, up, core_gate, core_up) in enumerate(
        ((gate0, up0, core_gate0, core_up0), (gate1, up1, core_gate1, core_up1))
    ):
        for k, own, core in ((0, gate, core_gate), (1, up, core_up)):
            lanes = slice(k * PAIR + j * TILE, k * PAIR + (j + 1) * TILE)
            w_both[pl.ds(pl.multiple_of(g * ROWS, ROWS), ROWS), lanes] = own[...]
            w_both[pl.ds(pl.multiple_of((g ^ 1) * ROWS, ROWS), ROWS), lanes] = core[...]
            for q, piece in ((2, far), (3, far_core)):
                for part in range(4):
                    start = ((g ^ q) * 4 + (low ^ part)) * quarter
                    rows = pl.ds(pl.multiple_of((k * GRP + 2 * step + j) * quarter, quarter), quarter)
                    w_both[pl.ds(pl.multiple_of(start, quarter), quarter), lanes] = piece[part, rows, :]

    @pl.when(step == 0)
    def _():
        w_down[g] = down[...]
        w_down[g ^ 1] = core_down[...]
        for q, piece in ((2, far), (3, far_core)):
            for part in range(4):
                lanes = pl.ds(pl.multiple_of((low ^ part) * (D // 4), D // 4), D // 4)
                w_down[g ^ q, :, lanes] = piece[part, 2 * ROWS :, :].T
        out_sum[...] = jnp.zeros_like(out_sum)
        grad_sum[...] = jnp.zeros_like(grad_sum)

    @pl.loop(0, count // block_rows)
    def _(block):
        rows = pl.ds(pl.multiple_of(block * block_rows, block_rows), block_rows)
        both = dot_nn(second[rows, :], w_both[...])
        gate = both[:, :PAIR]
        up = both[:, PAIR:]
        downs = w_down[pl.ds(2 * step, 2)].reshape(PAIR, D)
        inner_grad = dot_nt(grad[rows, :], downs)
        sigmoid = jax.nn.sigmoid(gate)
        silu = gate * sigmoid
        inner = (silu * up).astype(bf16)
        inner_low[rows, :] = inner
        both_low[rows, :PAIR] = (inner_grad * up * (sigmoid + silu * (1.0 - sigmoid))).astype(bf16)
        both_low[rows, PAIR:] = (inner_grad * silu).astype(bf16)
        out_sum[rows, :] += dot_nn(inner, downs)
        grad_sum[rows, :] += dot_nt(both_low[rows, :], w_both[...])

    for x in range(2):
        for c in range(2):
            rows = pl.ds(pl.multiple_of((g ^ (2 * x + c)) * ROWS, ROWS), ROWS)
            part = dot_nn(second_t[rows, :], both_low[...]).astype(bf16)
            target = gu_kept if c == 0 else gu_sent
            for k in range(2):
                for j in range(2):
                    start = k * PAIR + j * TILE
                    target[x, k, j] = part[:, start : start + TILE]

    @pl.loop(0, D // ROWS)
    def _(block):
        rows = pl.ds(pl.multiple_of(block * ROWS, ROWS), ROWS)
        part = dot_nn(grad_t[rows, :], inner_low[...]).astype(bf16)
        dn_kept[0, rows, :] = jnp.where(odd, part[:, TILE:], part[:, :TILE])
        dn_sent[0, rows, :] = jnp.where(odd, part[:, :TILE], part[:, TILE:])

    @pl.when(step == 1)
    def _():
        out[...] = out_sum[...].astype(bf16)
        second_grad[...] = grad_sum[...].astype(bf16)


def after_kernel(
    residual, grad, gain, out0, out1, out2, sg0, sg1, sg2, outputs, residual_grad, residual_low, gain_grad
):
    @pl.when(pl.program_id(0) == 0)
    def _():
        gain_grad[...] = jnp.zeros_like(gain_grad)

    total = residual[...]
    outputs[...] = (
        total + (out0[...].astype(f32) + out1[...].astype(f32) + out2[...].astype(f32))
    ).astype(bf16)
    second_grad = sg0[...].astype(f32) + sg1[...].astype(f32) + sg2[...].astype(f32)
    inverse = rms_scale(total)
    unit = total * inverse
    gain_grad[...] += jnp.sum(second_grad * unit, axis=0, keepdims=True)
    back = grad[...].astype(f32) + norm_back(second_grad * gain[...], unit, inverse)
    residual_grad[...] = back
    residual_low[...] = back.astype(bf16)


def last_kernel(tokens, residual_grad, gain, fg0, fg1, input_grad, gain_grad):
    @pl.when(pl.program_id(0) == 0)
    def _():
        gain_grad[...] = jnp.zeros_like(gain_grad)

    inputs = tokens[...].astype(f32)
    first_grad = fg0[...].astype(f32) + fg1[...].astype(f32)
    inverse = rms_scale(inputs)
    unit = inputs * inverse
    gain_grad[...] += jnp.sum(first_grad * unit, axis=0, keepdims=True)
    input_grad[...] = (
        residual_grad[...] + norm_back(first_grad * gain[...], unit, inverse)
    ).astype(bf16)


def finish_kernel(gate, up, down, *refs):
    gate_out, up_out, down_out = refs[-3:]
    gate_out[...] = gate[...].astype(f32)
    up_out[...] = up[...].astype(f32)
    down_out[...] = down[...].astype(f32).T


def split_kernel(block, query, key, value):
    query[...] = block[:, :GROUP_Q].astype(f32)
    key[...] = block[:, GROUP_Q:GROUP_QK].astype(f32)
    value[...] = block[:, GROUP_QK:].astype(f32)


struct = jax.ShapeDtypeStruct


def whole(shape):
    return pl.BlockSpec(
        shape, lambda *at: (0,) * len(shape), pipeline_mode=pl.Buffered(buffer_count=1)
    )


def params(megabytes):
    return pltpu.CompilerParams(
        dimension_semantics=("arbitrary",), vmem_limit_bytes=megabytes * 1024 * 1024
    )


def cost(flops, bytes_accessed):
    return pl.CostEstimate(
        flops=int(flops), bytes_accessed=int(bytes_accessed), transcendentals=0
    )


def rows_spec(width, rows=BLOCK):
    return pl.BlockSpec((rows, width), lambda t, *_: (t, 0))


def lanes_spec(rows, width):
    return pl.BlockSpec((rows, width), lambda t, *_: (0, t))


def pack(place, w_query, w_key, w_value, w_out):
    width = GRP * GROUP_ALL + D
    return pl.pallas_call(
        pack_kernel,
        grid_spec=pltpu.PrefetchScalarGridSpec(
            num_scalar_prefetch=1,
            grid=(1,),
            in_specs=[whole((ROWS, H * HD)), whole((ROWS, KV * HD)), whole((ROWS, KV * HD)), whole((ROWS, D))],
            out_specs=[whole((ROWS, width)), whole((ROWS // 4, width))],
        ),
        out_shape=[struct((ROWS, width), bf16), struct((ROWS // 4, width), bf16)],
        compiler_params=params(60),
        cost_estimate=cost(1e5, 3e6),
        name="pack",
    )(place, w_query, w_key, w_value, w_out)


def quarters(place, w_gate, w_up, w_down):
    part = ROWS // 4
    rows = 2 * GRP * part + D // 4
    return pl.pallas_call(
        quarters_kernel,
        grid_spec=pltpu.PrefetchScalarGridSpec(
            num_scalar_prefetch=1,
            grid=(1,),
            in_specs=[
                pl.BlockSpec((part, FF), lambda t, p: (p[1], 0)),
                pl.BlockSpec((part, FF), lambda t, p: (p[1], 0)),
                pl.BlockSpec((FF // GRP, D // 4), lambda t, p: (0, p[1])),
            ],
            out_specs=[whole((rows, TILE))] * CHUNKS,
        ),
        out_shape=[struct((rows, TILE), bf16)] * CHUNKS,
        compiler_params=params(60),
        cost_estimate=cost(1e5, 4e6),
        name="quarters",
    )(place, w_gate, w_up, w_down)


def first_norm(tokens, grad, gain):
    count = tokens.shape[0]
    return pl.pallas_call(
        first_kernel,
        grid=(count // BLOCK,),
        in_specs=[rows_spec(D), rows_spec(D), whole((1, D))],
        out_specs=[rows_spec(D), lanes_spec(D, BLOCK), lanes_spec(D, BLOCK)],
        out_shape=[struct((count, D), bf16), struct((D, count), bf16), struct((D, count), bf16)],
        compiler_params=params(60),
        cost_estimate=cost(1e7, 1e7),
        name="first_norm",
    )(tokens, grad, gain)


def attend(part, place, first, pieces, cos, sin, gain, seg_col, seg_row, spread):
    count = first.shape[0]
    steps = GRP // 2
    own, core, far, far_core = pieces
    far_spec = pl.BlockSpec((4, ROWS // 4, GROUP_ALL), lambda t, p: (0, 0, part * steps + t))
    own_spec = pl.BlockSpec((ROWS, GROUP_ALL), lambda t, p: (0, part * steps + t))
    return pl.pallas_call(
        attend_kernel,
        grid_spec=pltpu.PrefetchScalarGridSpec(
            num_scalar_prefetch=1,
            grid=(steps,),
            in_specs=[
                whole((count, D)),
                own_spec,
                own_spec,
                far_spec,
                far_spec,
                whole((count, 128)),
                whole((count, 128)),
                whole((1, GROUP_QK)),
                whole((count, 1)),
                whole((1, count)),
                whole((GROUP_QK, GROUP_QK)),
            ],
            out_specs=[
                lanes_spec(count, GROUP_QK),
                lanes_spec(count, GROUP_QK),
                lanes_spec(count, GROUP_K),
                lanes_spec(count, GROUP_Q),
                lanes_spec(count, GROUP_Q),
                lanes_spec(D, GROUP_ALL),
            ],
            scratch_shapes=[
                pltpu.VMEM((count, count), f32),
                pltpu.VMEM((count, 2 * HD), bf16),
            ],
        ),
        out_shape=[
            struct((count, steps * GROUP_QK), f32),
            struct((count, steps * GROUP_QK), bf16),
            struct((count, steps * GROUP_K), bf16),
            struct((count, steps * GROUP_Q), bf16),
            struct((count, steps * GROUP_Q), f32),
            struct((D, steps * GROUP_ALL), bf16),
        ],
        compiler_params=params(60),
        cost_estimate=cost(1e10, 1.2e7),
        name="attend",
    )(place, first, own, core, far, far_core, cos, sin, gain, seg_col, seg_row, spread)


def middle(place, mixed, tokens, gain, pieces):
    count = tokens.shape[0]
    own, core, far, far_core = pieces
    one = pl.Buffered(buffer_count=1)
    own_spec = pl.BlockSpec((ROWS, D), lambda t, p: (0, 2), pipeline_mode=one)
    far_spec = pl.BlockSpec((4, ROWS // 4, D), lambda t, p: (0, 0, 2), pipeline_mode=one)
    return pl.pallas_call(
        middle_kernel,
        grid_spec=pltpu.PrefetchScalarGridSpec(
            num_scalar_prefetch=1,
            grid=(count // BLOCK,),
            in_specs=[
                rows_spec(D // 2),
                rows_spec(D // 2),
                rows_spec(D),
                whole((1, D)),
                own_spec,
                own_spec,
                far_spec,
                far_spec,
            ],
            out_specs=[rows_spec(D), rows_spec(D), lanes_spec(D, BLOCK), whole((D, D))],
        ),
        out_shape=[
            struct((count, D), f32),
            struct((count, D), bf16),
            struct((D, count), bf16),
            struct((D, D), bf16),
        ],
        compiler_params=params(60),
        cost_estimate=cost(2e9, 1.6e7),
        name="middle",
    )(place, *mixed, tokens, gain, own, core, far, far_core)


def ffn(place, second, second_t, grad, grad_t, weights, i):
    count = second.shape[0]
    (gate, up, core_gate, core_up, down, core_down), (far, far_core) = weights
    tile = [
        pl.BlockSpec((ROWS, TILE), lambda t, p, j=j: (0, (2 * t + j) * CHUNKS + i))
        for j in range(2)
    ]
    one = pl.Buffered(buffer_count=1)
    down_spec = pl.BlockSpec((TILE, D), lambda t, p: (i, 0), pipeline_mode=one)
    gu_spec = pl.BlockSpec((2, 2, 2, ROWS, TILE), lambda t, p: (0, 0, t, 0, 0))
    dn_spec = pl.BlockSpec((1, D, TILE), lambda t, p: (t ^ (p[0] >> 1), 0, 0))
    return pl.pallas_call(
        ffn_kernel,
        grid_spec=pltpu.PrefetchScalarGridSpec(
            num_scalar_prefetch=1,
            grid=(2,),
            in_specs=[
                whole((count, D)),
                whole((D, count)),
                whole((count, D)),
                whole((D, count)),
            ]
            + tile * 4
            + [whole(far.shape)] * 2
            + [down_spec] * 2,
            out_specs=[whole((count, D)), whole((count, D)), gu_spec, gu_spec, dn_spec, dn_spec],
            scratch_shapes=[
                pltpu.VMEM((D, 2 * PAIR), bf16),
                pltpu.VMEM((GRP, TILE, D), bf16),
                pltpu.VMEM((count, PAIR), bf16),
                pltpu.VMEM((count, 2 * PAIR), bf16),
                pltpu.VMEM((count, D), f32),
                pltpu.VMEM((count, D), f32),
            ],
        ),
        out_shape=[
            struct((count, D), bf16),
            struct((count, D), bf16),
            struct((2, 2, GRP, ROWS, TILE), bf16),
            struct((2, 2, GRP, ROWS, TILE), bf16),
            struct((2, D, TILE), bf16),
            struct((2, D, TILE), bf16),
        ],
        compiler_params=params(60),
        cost_estimate=cost(2.9e10, 3.6e7),
        name="ffn",
    )(
        place, second, second_t, grad, grad_t,
        gate, gate, up, up, core_gate, core_gate, core_up, core_up,
        far, far_core, down, core_down,
    )


def after_ffn(residual, grad, gain, outs, second_grads):
    count = residual.shape[0]
    return pl.pallas_call(
        after_kernel,
        grid=(count // BLOCK,),
        in_specs=[rows_spec(D), rows_spec(D), whole((1, D))] + [rows_spec(D)] * 6,
        out_specs=[rows_spec(D), rows_spec(D), rows_spec(D), whole((1, D))],
        out_shape=[
            struct((count, D), bf16),
            struct((count, D), f32),
            struct((count, D), bf16),
            struct((1, D), f32),
        ],
        compiler_params=params(60),
        cost_estimate=cost(2e7, 2.4e7),
        name="after_ffn",
    )(residual, grad, gain, *outs, *second_grads)


def attend_back(
    part, place, residual_low, w_out, weights, first_t, proj, qk_low, v_low, mixed, lse, cos, sin,
    gain, seg_col, seg_row, spread,
):
    count = residual_low.shape[0]
    steps = GRP // 2
    step_cols = lambda width, rows=count: pl.BlockSpec((rows, width), lambda t, p: (0, t))
    grad_spec = pl.BlockSpec((2, ROWS, GROUP_ALL), lambda t, p: (0, 0, t))
    return pl.pallas_call(
        attend_back_kernel,
        grid_spec=pltpu.PrefetchScalarGridSpec(
            num_scalar_prefetch=1,
            grid=(steps,),
            in_specs=[
                whole((count, D)),
                pl.BlockSpec((ROWS, D), lambda t, p: (part * steps + t, 0)),
                step_cols(GROUP_ALL, D),
                whole((D, count)),
                step_cols(GROUP_QK),
                step_cols(GROUP_QK),
                step_cols(GROUP_K),
                step_cols(GROUP_Q),
                step_cols(GROUP_Q),
                whole((count, 128)),
                whole((count, 128)),
                whole((1, GROUP_QK)),
                whole((count, 1)),
                whole((1, count)),
                whole((GROUP_QK, GROUP_QK)),
            ],
            out_specs=[whole((count, D)), grad_spec, grad_spec, whole((1, GROUP_QK))],
            scratch_shapes=[
                pltpu.VMEM((count, count), f32),
                pltpu.VMEM((count, GROUP_Q), bf16),
                pltpu.VMEM((count, GROUP_Q), f32),
                pltpu.VMEM((count, GROUP_QK), f32),
                pltpu.VMEM((count, 2 * HD), f32),
                pltpu.VMEM((count, 2 * HD), f32),
                pltpu.VMEM((count, GROUP_ALL), bf16),
                pltpu.VMEM((count, 2 * HD), bf16),
                pltpu.VMEM((count, 2 * HD), bf16),
                pltpu.VMEM((count, D), f32),
            ],
        ),
        out_shape=[
            struct((count, D), bf16),
            struct((2, ROWS, steps * GROUP_ALL), bf16),
            struct((2, ROWS, steps * GROUP_ALL), bf16),
            struct((1, GROUP_QK), f32),
        ],
        compiler_params=params(60),
        cost_estimate=cost(3e10, 2e7),
        name="attend_back",
    )(
        place, residual_low, w_out, weights, first_t, proj, qk_low, v_low, mixed, lse, cos, sin,
        gain, seg_col, seg_row, spread,
    )


def last_norm(tokens, residual_grad, gain, first_grads):
    count = tokens.shape[0]
    return pl.pallas_call(
        last_kernel,
        grid=(count // BLOCK,),
        in_specs=[rows_spec(D), rows_spec(D), whole((1, D)), rows_spec(D), rows_spec(D)],
        out_specs=[rows_spec(D), whole((1, D))],
        out_shape=[struct((count, D), bf16), struct((1, D), f32)],
        compiler_params=params(60),
        cost_estimate=cost(2e7, 1.2e7),
        name="last_norm",
    )(tokens, residual_grad, gain, *first_grads)


def finish(i, total, held):
    both_spec = pl.BlockSpec((ROWS, TILE), lambda t: (0, t * CHUNKS + i))
    any_spec = pl.BlockSpec(memory_space=pl.ANY)
    return pl.pallas_call(
        finish_kernel,
        grid=(GRP,),
        in_specs=[
            pl.BlockSpec((ROWS, TILE), lambda t: (t, 0)),
            pl.BlockSpec((ROWS, TILE), lambda t: (GRP + t, 0)),
            pl.BlockSpec((ROWS, TILE), lambda t: (2 * GRP + t, 0)),
        ]
        + [any_spec] * len(held),
        out_specs=[both_spec, both_spec, pl.BlockSpec((TILE, ROWS), lambda t: (i, t))],
        out_shape=[
            struct((ROWS, FF), f32),
            struct((ROWS, FF), f32),
            struct((FF // GRP, D), f32),
        ],
        input_output_aliases={3 + k: k for k in range(len(held))},
        compiler_params=params(60),
        cost_estimate=cost(1e6, 8e6),
        name="finish",
    )(total, total, total, *held)


def split_sums(halves):
    def one(half, held):
        at = lambda width: pl.BlockSpec((ROWS, width), lambda t: (0, GRP // 2 * half + t))
        return pl.pallas_call(
            lambda block, *refs: split_kernel(block, *refs[-3:]),
            grid=(GRP // 2,),
            in_specs=[lanes_spec(ROWS, GROUP_ALL)]
            + [pl.BlockSpec(memory_space=pl.ANY)] * len(held),
            out_specs=[at(GROUP_Q), at(GROUP_K), at(GROUP_K)],
            out_shape=[
                struct((ROWS, H * HD), f32),
                struct((ROWS, KV * HD), f32),
                struct((ROWS, KV * HD), f32),
            ],
            input_output_aliases={1 + k: k for k in range(len(held))},
            compiler_params=params(60),
            cost_estimate=cost(1e6, 4e6),
            name="split_sums",
        )(halves[half], *held)

    return one(1, one(0, ()))


class Job:
    def __init__(self, stages):
        self.stages, self.done, self.result = stages, False, None
        self.advance(None)

    def advance(self, came):
        try:
            self.wanted = self.stages.send(came)
        except StopIteration as stop:
            self.done, self.wanted, self.result = True, [], stop.value

    def start(self, payloads):
        self.flight = [send(values) for values, (_, send) in zip(payloads, self.wanted)]


def on_device(rep_count):
    core_pairs = [(i, i ^ 1) for i in range(GRP)]
    far_pairs = [(i, i ^ 2) for i in range(GRP)]
    rep_bits = rep_count.bit_length() - 1

    def to_core(values):
        return lax.ppermute(values, "grp", core_pairs)

    def to_far(values):
        return lax.ppermute(values, "grp", far_pairs)

    def by_xor(mask):
        pairs = [(i, i ^ mask) for i in range(rep_count)]
        return lambda values: lax.ppermute(values, "rep", pairs)

    def to_rep(bit):
        return by_xor(1 << bit)

    def ordered(upper, own, other):
        return jnp.concatenate([jnp.where(upper, other, own), jnp.where(upper, own, other)], axis=0)

    def low_sum(terms):
        return sum(term.astype(f32) for term in terms).astype(bf16)

    def half_of(values, upper, axis=0):
        half = values.shape[axis] // 2
        return lax.dynamic_slice_in_dim(values, upper * half, half, axis)

    def reduce_stages(kept, sent, early=()):
        rep = lax.axis_index("rep")
        upper_of = lambda bit: (rep >> bit) & 1
        flat = lambda values: values.reshape(-1, values.shape[-1])
        wide = lambda values: values.reshape(2, -1, values.shape[-1])
        join = lambda parts, axis=0: jnp.concatenate(parts, axis=axis) if len(parts) > 1 else parts[0]
        came = yield [(values, to_core) for values in sent]
        if early:
            both = join(
                [low_sum([wide(mine), wide(other)]) for mine, other in zip(kept, came)], axis=1
            )
            terms = [both]
            for bit in early:
                upper = upper_of(bit)
                away = low_sum([half_of(term, 1 - upper, 1) for term in terms])
                terms = [half_of(term, upper, 1) for term in terms]
                terms += yield [(away, to_rep(bit))]
            away = low_sum([term[1] for term in terms])
            terms = [term[0] for term in terms]
        else:
            away = join(
                [low_sum([flat(mine[1]), flat(other[1])]) for mine, other in zip(kept, came)]
            )
            terms = [
                join([flat(values[0]) for values in kept]),
                join([flat(values[0]) for values in came]),
            ]
        terms += yield [(away, to_far)]
        late = [bit for bit in range(rep_bits) if bit not in early]
        for bit in late:
            upper = upper_of(bit)
            away = low_sum([half_of(term, 1 - upper) for term in terms])
            terms = [half_of(term, upper) for term in terms]
            terms += yield [(away, to_rep(bit))]
        total = low_sum(terms)
        for bit in reversed(list(early) + late):
            (got,) = yield [(total, to_rep(bit))]
            total = ordered(upper_of(bit) == 1, total, got)
        return total

    def small_stages(values):
        for send in [to_core, to_far] + [to_rep(bit) for bit in range(rep_bits)]:
            (got,) = yield [(values, send)]
            values = values + got
        return values

    def beside(run, inputs, starting, ending):
        starting = [job for job in starting if not job.done]
        ending = [job for job in ending if not job.done]
        payloads = [[values for values, _ in job.wanted] for job in starting]
        inputs, payloads = tie(tuple(inputs), payloads)
        for job, group in zip(starting, payloads):
            job.start(group)
        outs = run(*inputs)
        outs, came = tie(outs, [job.flight for job in ending])
        for job, group in zip(ending, came):
            job.advance(group)
        return outs

    def finish_jobs(jobs):
        while not all(job.done for job in jobs):
            left = [job for job in jobs if not job.done]
            payloads = tie(*[[values for values, _ in job.wanted] for job in left])
            for job, group in zip(left, payloads):
                job.start(group)
            for job, group in zip(left, tie(*[job.flight for job in left])):
                job.advance(group)
        return [job.result for job in jobs]

    def body(
        tokens, segments, attn_gain, w_query, w_key, w_value, query_gain, key_gain, w_out, ffn_gain,
        w_gate, w_up, w_down, out_grad,
    ):
        count = tokens.shape[0]
        g = lax.axis_index("grp").astype(jnp.int32)
        low = (lax.axis_index("rep") & 3).astype(jnp.int32)
        place = jnp.stack([g, low])

        to_y, to_z = to_rep(0), to_rep(1)

        def spread_one(quarter):
            return to_y(quarter), to_z(quarter)

        def spread_two(by_y, by_z):
            half = by_y.shape[0] // 2
            return to_z(by_y[:half]), to_y(by_z[half:])

        def far_of(quarter, by_y, by_z, first_half, second_half):
            return jnp.stack(
                [quarter, by_y, by_z, jnp.concatenate([first_half, second_half], axis=0)]
            )

        gains = jnp.concatenate([attn_gain, ffn_gain, query_gain, key_gain, jnp.zeros((96,), bf16)])
        own_attn, q_attn = pack(place, w_query, w_key, w_value, w_out)

        given, q_attn = tie((place, w_gate, w_up, w_down, segments), q_attn)
        x_attn = to_far(q_attn)
        q_ffn = quarters(*given[:4])
        gains = lax.all_gather(gains, "grp", axis=0, tiled=False).astype(f32)
        attn_full = gains[:, :ROWS].reshape(1, D)
        ffn_full = gains[:, ROWS : 2 * ROWS].reshape(1, D)
        query_full = gains[:, 2 * ROWS : 2 * ROWS + 16].reshape(1, HD)
        key_full = gains[:, 2 * ROWS + 16 : 2 * ROWS + 32].reshape(1, HD)
        x_attn, q_ffn, attn_full, segments = tie(x_attn, q_ffn, attn_full, given[4])

        yz_attn, x0 = spread_one(x_attn), to_far(q_ffn[0])
        core_attn = to_core(own_attn)
        first, first_t, grad_t = first_norm(tokens, out_grad, attn_full)
        yz_attn, x0, core_attn, first, segments = tie(yz_attn, x0, core_attn, first, segments)

        two_attn, x1 = spread_two(*yz_attn), to_far(q_ffn[1])
        places = jnp.arange(count, dtype=jnp.int32)
        seg_col = segments.reshape(count, 1)
        seg_row = segments.reshape(1, count)
        keep = (seg_col == seg_row) & (places[None, :] <= places[:, None])
        position = (jnp.sum(keep.astype(jnp.int32), axis=1) - 1).astype(f32)
        freqs = theta_base ** (-(2.0 * jnp.arange(HD // 2, dtype=f32)) / HD)
        angles = position[:, None] * freqs[None, :]
        cos, sin = jnp.cos(angles), jnp.sin(angles)
        cos = jnp.concatenate([cos, cos, cos, cos], axis=1)
        sin = jnp.concatenate([-sin, sin, -sin, sin], axis=1)
        lane = jnp.arange(GROUP_QK, dtype=jnp.int32) // HD
        spread = jnp.where(lane[:, None] == lane[None, :], 1.0 / HD, 0.0).astype(bf16)
        head_gain = jnp.concatenate([query_full] * (H // GRP) + [key_full] * (KV // GRP), axis=1)
        fold = jnp.where(jnp.arange(GROUP_QK) < GROUP_Q, score_scale * log2_e, 1.0)[None, :]
        two_attn, x1, cos, sin, spread, head_gain = tie(two_attn, x1, cos, sin, spread, head_gain)

        far_attn = far_of(x_attn, *yz_attn, *two_attn)
        far_core_attn = to_core(far_attn)
        attn_pieces = (own_attn, core_attn, far_attn, far_core_attn)
        inputs = (place, first, attn_pieces, cos, sin, head_gain * fold, seg_col, seg_row, spread)
        inputs, x0, x1, q2 = tie(inputs, x0, x1, q_ffn[2])
        yz0, x2 = spread_one(x0), to_far(q2)
        saved0, inputs, yz0, x1, x2, owns = tie(
            attend(0, *inputs), inputs, yz0, x1, x2, [w_gate, w_up, w_down]
        )
        two0, yz1, yz2 = spread_two(*yz0), spread_one(x1), spread_one(x2)
        cores = [to_core(values) for values in owns]
        saved1, two0, yz1, yz2, cores = tie(attend(1, *inputs), two0, yz1, yz2, cores)
        far0 = far_of(x0, *yz0, *two0)
        mixed = (saved0[3], saved1[3])
        far0, yz1, yz2, mixed = tie(far0, yz1, yz2, mixed)
        two1, two2 = spread_two(*yz1), spread_two(*yz2)
        far_core0 = to_core(far0)
        middle_out, far_core0, two1, two2 = tie(
            middle(place, mixed, tokens, ffn_full, attn_pieces), far_core0, two1, two2
        )
        residual, second, second_t, out_weights = middle_out
        far1, far2 = far_of(x1, *yz1, *two1), far_of(x2, *yz2, *two2)
        second, far1, far2 = tie(second, far1, far2)
        core_gate, core_up, core_down = cores
        near = (w_gate, w_up, core_gate, core_up, w_down, core_down)
        fars = [(far0, far_core0), None, None]

        outs, second_grads, jobs = [], [], []
        for i in range(CHUNKS):
            (out, second_grad, gu_kept, gu_sent, dn_kept, dn_sent) = beside(
                lambda *given, i=i: ffn(*given, i),
                (place, second, second_t, out_grad, grad_t, (near, fars[i])),
                jobs,
                jobs,
            )
            if i == 0:
                out, *far_cores = tie(out, to_core(far1), to_core(far2))
                fars[1:] = [(far1, far_cores[0]), (far2, far_cores[1])]
            outs.append(out)
            second_grads.append(second_grad)
            early = (1,) if i == CHUNKS - 1 else ()
            jobs.append(Job(reduce_stages([gu_kept, dn_kept], [gu_sent, dn_sent], early)))

        outputs, residual_grad, residual_low, ffn_gain_grad = beside(
            after_ffn, (residual, out_grad, ffn_full, outs, second_grads), jobs[2:], jobs[2:]
        )

        def out_back(mixed, residual_low):
            wgrad = dot_tn(jnp.concatenate(mixed, axis=1), residual_low)
            wgrad = wgrad.astype(bf16).reshape(GRP, ROWS, D)
            at = lambda q: lax.dynamic_slice_in_dim(wgrad, g ^ q, 1, 0)
            return jnp.concatenate([at(0), at(2)], axis=0), jnp.concatenate([at(1), at(3)], axis=0)

        out_kept, out_sent = out_back(mixed, residual_low)
        jobs.append(Job(reduce_stages([out_kept], [out_sent])))

        first_grads, head_grads = [], []
        for part, saved in enumerate((saved0, saved1)):
            first_grad, kept, sent, head_grad = beside(
                lambda *given, part=part: attend_back(part, *given),
                (
                    place, residual_low, out_weights, saved[5], first_t, *saved[:5],
                    cos, sin, head_gain, seg_col, seg_row, spread,
                ),
                jobs,
                jobs,
            )
            first_grads.append(first_grad)
            head_grads.append(head_grad)
            jobs.append(Job(reduce_stages([kept], [sent])))
        input_grad, attn_gain_grad = beside(
            last_norm, (tokens, residual_grad, attn_full, first_grads), jobs, jobs
        )

        head_grad = (head_grads[0] + head_grads[1]).reshape(GROUP_QK // HD, HD)
        small = jnp.concatenate(
            [
                attn_gain_grad[0],
                ffn_gain_grad[0],
                jnp.sum(head_grad[: GROUP_Q // HD], axis=0),
                jnp.sum(head_grad[GROUP_Q // HD :], axis=0),
            ]
        )
        jobs.append(Job(small_stages(small.reshape(1, -1))))
        sum0, sum1, sum2, out_sum, attn0, attn1, small = finish_jobs(jobs)
        mine = lambda start, size: lax.dynamic_slice_in_dim(small[0], start + g * size, size, 0)
        held = ()
        for i, total in enumerate((sum0, sum1, sum2)):
            held = finish(i, total, held)
        gate_grad, up_grad, down_grad = held
        query_grad, key_grad, value_grad = split_sums((attn0, attn1))
        return (
            outputs,
            input_grad,
            mine(0, ROWS),
            query_grad,
            key_grad,
            value_grad,
            mine(2 * D, HD // GRP),
            mine(2 * D + HD, HD // GRP),
            out_sum.astype(f32),
            mine(D, ROWS),
            gate_grad,
            up_grad,
            down_grad,
        )

    return body


def solution(mesh):
    tokens_spec, weight_spec, vector_spec = P(("rep", "grp"), None), P("grp", None), P("grp")
    return jax.shard_map(
        on_device(mesh.shape["rep"]),
        mesh=mesh,
        in_specs=(
            tokens_spec,
            P(("rep", "grp")),
            vector_spec,
            weight_spec,
            weight_spec,
            weight_spec,
            vector_spec,
            vector_spec,
            weight_spec,
            vector_spec,
            weight_spec,
            weight_spec,
            weight_spec,
            tokens_spec,
        ),
        out_specs=(
            tokens_spec,
            tokens_spec,
            vector_spec,
            weight_spec,
            weight_spec,
            weight_spec,
            vector_spec,
            vector_spec,
            weight_spec,
            vector_spec,
            weight_spec,
            weight_spec,
            weight_spec,
        ),
        check_vma=False,
    )
```

```python
import functools

import jax
import jax.numpy as jnp
from jax import lax
from jax.experimental import pallas as pl
from jax.experimental.pallas import tpu as pltpu
from jax.sharding import PartitionSpec as P

D = 1024
H = 16
KV = 8
HD = 64
FF = 4608
SEQ = 1024
GRP = 4
CHUNKS = 3
TILE = FF // GRP // CHUNKS
ROWS = D // GRP
PAIR = 2 * TILE
GROUP_Q = H // GRP * HD
GROUP_K = KV // GRP * HD
GROUP_QK = GROUP_Q + GROUP_K
GROUP_ALL = GROUP_QK + GROUP_K
BLOCK = 256

epsilon = 1e-05
theta_base = 1000000.0
score_scale = HD ** (-0.5)
log2_e = 1.4426950408889634
ln_2 = 0.6931471805599453

f32 = jnp.float32
bf16 = jnp.bfloat16


def dot_nn(left, right):
    return lax.dot_general(left, right, (((1,), (0,)), ((), ())), preferred_element_type=f32)


def dot_nt(left, right):
    return lax.dot_general(left, right, (((1,), (1,)), ((), ())), preferred_element_type=f32)


def dot_tn(left, right):
    return lax.dot_general(left, right, (((0,), (0,)), ((), ())), preferred_element_type=f32)


def rms_scale(values):
    return lax.rsqrt(jnp.mean(values * values, axis=-1, keepdims=True) + epsilon)


def norm_back(grad_unit, unit, inverse):
    return inverse * (grad_unit - unit * jnp.mean(grad_unit * unit, axis=-1, keepdims=True))


def block_of(ref, block, rows):
    return ref.at[pl.ds(pl.multiple_of(block * rows, rows), rows)]


def tie(*values):
    return lax.optimization_barrier(values)


def split_two(values):
    high = values.astype(bf16)
    return high, (values - high.astype(f32)).astype(bf16)


def head_mean(values, spread):
    high, rest = split_two(values)
    return dot_nn(high, spread) + dot_nn(rest, spread)


def swap_halves(values):
    width = values.shape[-1]
    lane = lax.broadcasted_iota(jnp.int32, values.shape, 1)
    ahead = pltpu.roll(values, width - 32, 1)
    behind = pltpu.roll(values, 32, 1)
    return jnp.where((lane & 63) < 32, ahead, behind)


def three_lanes(values):
    high = values.astype(bf16).astype(f32)
    rest = values - high
    mid = rest.astype(bf16).astype(f32)
    lane = lax.broadcasted_iota(jnp.int32, values.shape, 1)
    out = jnp.where(lane == 0, high, jnp.where(lane == 1, mid, jnp.where(lane == 2, rest - mid, 0.0)))
    return out.astype(bf16)


def three_ones(rows):
    lane = lax.broadcasted_iota(jnp.int32, (rows, HD), 1)
    return jnp.where(lane < 3, 1.0, 0.0).astype(bf16)


def fill_mask(mask, seg_col, seg_row):
    count = mask.shape[0]
    for start in range(0, count, BLOCK):
        rows = lax.broadcasted_iota(jnp.int32, (BLOCK, count), 0) + start
        cols = lax.broadcasted_iota(jnp.int32, (BLOCK, count), 1)
        keep = (seg_col[start : start + BLOCK, :] == seg_row[...]) & (cols <= rows)
        mask[start : start + BLOCK, :] = jnp.where(keep, 1.0, 0.0)


def place_rows(place_ref, held, pieces, start=0, stop=None):
    own, core, far, far_core = pieces
    g, low = place_ref[0], place_ref[1]
    rows = held.shape[0] // GRP
    quarter = rows // 4
    block_of(held, g, rows)[...] = own
    block_of(held, g ^ 1, rows)[...] = core
    for q, piece in ((2, far), (3, far_core)):
        for k in range(4):
            block_of(held, (g ^ q) * 4 + (low ^ k), quarter)[...] = piece[k]


def pack_kernel(place_ref, w_query, w_key, w_value, w_out, out, quarter):
    for a in range(GRP):
        start = a * GROUP_ALL
        out[:, start : start + GROUP_Q] = w_query[:, a * GROUP_Q : (a + 1) * GROUP_Q]
        out[:, start + GROUP_Q : start + GROUP_QK] = w_key[:, a * GROUP_K : (a + 1) * GROUP_K]
        out[:, start + GROUP_QK : start + GROUP_ALL] = w_value[:, a * GROUP_K : (a + 1) * GROUP_K]
    out[:, GRP * GROUP_ALL :] = w_out[...]
    quarter[...] = block_of(out, place_ref[1], ROWS // 4)[...]


def quarters_kernel(place_ref, gate, up, down, *outs):
    part = ROWS // 4
    for i, out in enumerate(outs):
        for k, weight in ((0, gate), (1, up)):
            for a in range(GRP):
                first = (a * CHUNKS + i) * TILE
                start = (k * GRP + a) * part
                out[start : start + part, :] = weight[:, first : first + TILE]
        out[2 * GRP * part :, :] = down[i * TILE : (i + 1) * TILE, :].T


def first_kernel(tokens, grad, gain, first, first_t, grad_t):
    inputs = tokens[...].astype(f32)
    low = (inputs * rms_scale(inputs) * gain[...]).astype(bf16)
    first[...] = low
    first_t[...] = low.T
    grad_t[...] = grad[...].T


def attend_kernel(
    place_ref, first, own, core, far, far_core, cos, sin, gain, seg_col, seg_row, spread,
    proj, qk_low, v_low, mixed, lse, weights, mask, ones_v,
):
    count = first.shape[0]
    place_rows(place_ref, weights, (own[...], core[...], far, far_core))

    @pl.when(pl.program_id(0) == 0)
    def _():
        fill_mask(mask, seg_col, seg_row)

    @pl.loop(0, count // BLOCK)
    def _(block):
        rows = pl.ds(pl.multiple_of(block * BLOCK, BLOCK), BLOCK)
        values = dot_nn(first[rows, :], weights[...])
        qk = values[:, :GROUP_QK]
        proj[rows, :] = qk
        inverse = lax.rsqrt(head_mean(qk * qk, spread[...]) + epsilon)
        normed = qk * inverse * gain[...]
        cos_rows = jnp.concatenate([cos[rows, :]] * (GROUP_QK // 128), axis=1)
        sin_rows = jnp.concatenate([sin[rows, :]] * (GROUP_QK // 128), axis=1)
        qk_low[rows, :] = (normed * cos_rows + swap_halves(normed) * sin_rows).astype(bf16)
        v_low[rows, :] = values[:, GROUP_QK:].astype(bf16)

    for j in range(GROUP_K // HD):
        ones_v[:, :HD] = v_low[:, j * HD : (j + 1) * HD]
        ones_v[:, HD:] = jnp.ones((count, HD), bf16)
        keys = qk_low[:, GROUP_Q + j * HD : GROUP_Q + (j + 1) * HD]
        for start in range(0, count, BLOCK):
            stop = start + BLOCK
            pair = jnp.concatenate(
                [
                    qk_low[start:stop, (2 * j + i) * HD : (2 * j + i + 1) * HD]
                    for i in range(2)
                ],
                axis=0,
            )
            scores = dot_nt(pair, keys[:stop])
            keep = mask[start:stop, :stop]
            weights_low = (jnp.exp2(scores) * jnp.concatenate([keep, keep], axis=0)).astype(bf16)
            summed = dot_nn(weights_low, ones_v[:stop, :])
            total = summed[:, HD:]
            part = (summed[:, :HD] / total).astype(bf16)
            log_total = jnp.log2(total)
            for i in range(2):
                lanes = slice((2 * j + i) * HD, (2 * j + i + 1) * HD)
                mixed[start:stop, lanes] = part[i * BLOCK : (i + 1) * BLOCK]
                lse[start:stop, lanes] = log_total[i * BLOCK : (i + 1) * BLOCK]


def attend_back_kernel(
    place_ref, residual_low, w_out, weights, first_t, proj, qk_low, v_low, mixed, lse, cos, sin, gain,
    seg_col, seg_row, spread,
    first_low, kept, sent, gain_grad,
    mask, mixed_grad, delta, grads, key_grad, value_grad, low_grads, key_ext, value_ext, first_grad,
):
    count = residual_low.shape[0]
    step = pl.program_id(0)

    @pl.when(step == 0)
    def _():
        fill_mask(mask, seg_col, seg_row)
        first_grad[...] = jnp.zeros_like(first_grad)
        gain_grad[...] = jnp.zeros_like(gain_grad)

    @pl.loop(0, count // BLOCK)
    def _(block):
        rows = pl.ds(pl.multiple_of(block * BLOCK, BLOCK), BLOCK)
        low = dot_nt(residual_low[rows, :], w_out[...]).astype(bf16)
        mixed_grad[rows, :] = low
        product = low.astype(f32) * mixed[rows, :].astype(f32)
        delta[rows, :] = head_mean(product, spread[:GROUP_Q, :GROUP_Q]) * HD

    for j in range(GROUP_K // HD):
        key_ext[:, :HD] = qk_low[:, GROUP_Q + j * HD : GROUP_Q + (j + 1) * HD]
        key_ext[:, HD:] = three_ones(count)
        value_ext[:, :HD] = v_low[:, j * HD : (j + 1) * HD]
        value_ext[:, HD:] = three_ones(count)
        key_grad[...] = jnp.zeros_like(key_grad)
        value_grad[...] = jnp.zeros_like(value_grad)
        for start in range(0, count, BLOCK):
            stop = start + BLOCK
            query_rows, grad_rows = [], []
            for i in range(2):
                lanes = slice((2 * j + i) * HD, (2 * j + i + 1) * HD)
                query_rows.append(
                    jnp.concatenate(
                        [qk_low[start:stop, lanes], three_lanes(-lse[start:stop, lanes])], axis=1
                    )
                )
                grad_rows.append(
                    jnp.concatenate(
                        [mixed_grad[start:stop, lanes], three_lanes(-delta[start:stop, lanes])],
                        axis=1,
                    )
                )
            query_ext = jnp.concatenate(query_rows, axis=0)
            grad_ext = jnp.concatenate(grad_rows, axis=0)
            keep = mask[start:stop, :stop]
            probs = jnp.exp2(dot_nt(query_ext, key_ext[:stop, :])) * jnp.concatenate(
                [keep, keep], axis=0
            )
            score_grad = (probs * dot_nt(grad_ext, value_ext[:stop, :])).astype(bf16)
            query_grad = dot_nn(score_grad, key_ext[:stop, :]) * score_scale
            for i in range(2):
                lanes = slice((2 * j + i) * HD, (2 * j + i + 1) * HD)
                grads[start:stop, lanes] = query_grad[i * BLOCK : (i + 1) * BLOCK, :HD]
            key_grad[:stop, :] += dot_tn(score_grad, query_ext)
            value_grad[:stop, :] += dot_tn(probs.astype(bf16), grad_ext)
        grads[:, GROUP_Q + j * HD : GROUP_Q + (j + 1) * HD] = key_grad[:, :HD] * ln_2
        low_grads[:, GROUP_QK + j * HD : GROUP_QK + (j + 1) * HD] = value_grad[:, :HD].astype(bf16)

    @pl.loop(0, count // BLOCK)
    def _(block):
        rows = pl.ds(pl.multiple_of(block * BLOCK, BLOCK), BLOCK)
        cos_rows = jnp.concatenate([cos[rows, :]] * (GROUP_QK // 128), axis=1)
        sin_rows = jnp.concatenate([sin[rows, :]] * (GROUP_QK // 128), axis=1)
        turned = grads[rows, :]
        turned = turned * cos_rows - swap_halves(turned) * sin_rows
        qk = proj[rows, :]
        inverse = lax.rsqrt(head_mean(qk * qk, spread[...]) + epsilon)
        unit = qk * inverse
        gain_grad[...] += jnp.sum(turned * unit, axis=0, keepdims=True)
        scaled = turned * gain[...]
        back = inverse * (scaled - unit * head_mean(scaled * unit, spread[...]))
        low_grads[rows, :GROUP_QK] = back.astype(bf16)
        first_grad[rows, :] += dot_nt(low_grads[rows, :], weights[...])

    for x in range(2):
        for c in range(2):
            rows = pl.ds(pl.multiple_of((place_ref[0] ^ (2 * x + c)) * ROWS, ROWS), ROWS)
            part = dot_nn(first_t[rows, :], low_grads[...]).astype(bf16)
            if c == 0:
                kept[x] = part
            else:
                sent[x] = part

    @pl.when(step == pl.num_programs(0) - 1)
    def _():
        first_low[...] = first_grad[...].astype(bf16)


def middle_kernel(
    place_ref, mixed0, mixed1, tokens, gain, own, core, far, far_core, residual, second, second_t, w_out
):
    @pl.when(pl.program_id(0) == 0)
    def _():
        place_rows(place_ref, w_out, (own[...], core[...], far, far_core))

    mixed = jnp.concatenate([mixed0[...], mixed1[...]], axis=1)
    total = tokens[...].astype(f32) + dot_nn(mixed, w_out[...])
    residual[...] = total
    low = (total * rms_scale(total) * gain[...]).astype(bf16)
    second[...] = low
    second_t[...] = low.T


def ffn_kernel(
    place_ref, second, second_t, grad, grad_t,
    gate0, gate1, up0, up1, core_gate0, core_gate1, core_up0, core_up1, far, far_core,
    down, core_down,
    out, second_grad, gu_kept, gu_sent, dn_kept, dn_sent,
    w_both, w_down, inner_low, both_low, out_sum, grad_sum,
):
    step = pl.program_id(0)
    g, low = place_ref[0], place_ref[1]
    odd = (g & 1) == 1
    count = second.shape[0]
    block_rows = min(512, count)
    quarter = ROWS // 4
    for j, (gate, up, core_gate, core_up) in enumerate(
        ((gate0, up0, core_gate0, core_up0), (gate1, up1, core_gate1, core_up1))
    ):
        for k, own, core in ((0, gate, core_gate), (1, up, core_up)):
            lanes = slice(k * PAIR + j * TILE, k * PAIR + (j + 1) * TILE)
            w_both[pl.ds(pl.multiple_of(g * ROWS, ROWS), ROWS), lanes] = own[...]
            w_both[pl.ds(pl.multiple_of((g ^ 1) * ROWS, ROWS), ROWS), lanes] = core[...]
            for q, piece in ((2, far), (3, far_core)):
                for part in range(4):
                    start = ((g ^ q) * 4 + (low ^ part)) * quarter
                    rows = pl.ds(pl.multiple_of((k * GRP + 2 * step + j) * quarter, quarter), quarter)
                    w_both[pl.ds(pl.multiple_of(start, quarter), quarter), lanes] = piece[part, rows, :]

    @pl.when(step == 0)
    def _():
        w_down[g] = down[...]
        w_down[g ^ 1] = core_down[...]
        for q, piece in ((2, far), (3, far_core)):
            for part in range(4):
                lanes = pl.ds(pl.multiple_of((low ^ part) * (D // 4), D // 4), D // 4)
                w_down[g ^ q, :, lanes] = piece[part, 2 * ROWS :, :].T
        out_sum[...] = jnp.zeros_like(out_sum)
        grad_sum[...] = jnp.zeros_like(grad_sum)

    @pl.loop(0, count // block_rows)
    def _(block):
        rows = pl.ds(pl.multiple_of(block * block_rows, block_rows), block_rows)
        both = dot_nn(second[rows, :], w_both[...])
        gate = both[:, :PAIR]
        up = both[:, PAIR:]
        downs = w_down[pl.ds(2 * step, 2)].reshape(PAIR, D)
        inner_grad = dot_nt(grad[rows, :], downs)
        sigmoid = jax.nn.sigmoid(gate)
        silu = gate * sigmoid
        inner = (silu * up).astype(bf16)
        inner_low[rows, :] = inner
        both_low[rows, :PAIR] = (inner_grad * up * (sigmoid + silu * (1.0 - sigmoid))).astype(bf16)
        both_low[rows, PAIR:] = (inner_grad * silu).astype(bf16)
        out_sum[rows, :] += dot_nn(inner, downs)
        grad_sum[rows, :] += dot_nt(both_low[rows, :], w_both[...])

    for x in range(2):
        for c in range(2):
            rows = pl.ds(pl.multiple_of((g ^ (2 * x + c)) * ROWS, ROWS), ROWS)
            part = dot_nn(second_t[rows, :], both_low[...]).astype(bf16)
            target = gu_kept if c == 0 else gu_sent
            for k in range(2):
                for j in range(2):
                    start = k * PAIR + j * TILE
                    target[x, k, j] = part[:, start : start + TILE]

    @pl.loop(0, D // ROWS)
    def _(block):
        rows = pl.ds(pl.multiple_of(block * ROWS, ROWS), ROWS)
        part = dot_nn(grad_t[rows, :], inner_low[...]).astype(bf16)
        dn_kept[0, rows, :] = jnp.where(odd, part[:, TILE:], part[:, :TILE])
        dn_sent[0, rows, :] = jnp.where(odd, part[:, :TILE], part[:, TILE:])

    @pl.when(step == 1)
    def _():
        out[...] = out_sum[...].astype(bf16)
        second_grad[...] = grad_sum[...].astype(bf16)


def after_kernel(
    residual, grad, gain, out0, out1, out2, sg0, sg1, sg2, outputs, residual_grad, residual_low, gain_grad
):
    @pl.when(pl.program_id(0) == 0)
    def _():
        gain_grad[...] = jnp.zeros_like(gain_grad)

    total = residual[...]
    outputs[...] = (
        total + (out0[...].astype(f32) + out1[...].astype(f32) + out2[...].astype(f32))
    ).astype(bf16)
    second_grad = sg0[...].astype(f32) + sg1[...].astype(f32) + sg2[...].astype(f32)
    inverse = rms_scale(total)
    unit = total * inverse
    gain_grad[...] += jnp.sum(second_grad * unit, axis=0, keepdims=True)
    back = grad[...].astype(f32) + norm_back(second_grad * gain[...], unit, inverse)
    residual_grad[...] = back
    residual_low[...] = back.astype(bf16)


def last_kernel(tokens, residual_grad, gain, *refs):
    *parts, input_grad, gain_grad = refs

    @pl.when(pl.program_id(0) == 0)
    def _():
        gain_grad[...] = jnp.zeros_like(gain_grad)

    inputs = tokens[...].astype(f32)
    first_grad = sum(part[...].astype(f32) for part in parts)
    inverse = rms_scale(inputs)
    unit = inputs * inverse
    gain_grad[...] += jnp.sum(first_grad * unit, axis=0, keepdims=True)
    input_grad[...] = (
        residual_grad[...] + norm_back(first_grad * gain[...], unit, inverse)
    ).astype(bf16)


def finish_kernel(gate, up, down, *refs):
    gate_out, up_out, down_out = refs[-3:]
    gate_out[...] = gate[...].astype(f32)
    up_out[...] = up[...].astype(f32)
    down_out[...] = down[...].astype(f32).T


def split_kernel(block, query, key, value):
    query[...] = block[:, :GROUP_Q].astype(f32)
    key[...] = block[:, GROUP_Q:GROUP_QK].astype(f32)
    value[...] = block[:, GROUP_QK:].astype(f32)


struct = jax.ShapeDtypeStruct


def whole(shape):
    return pl.BlockSpec(
        shape, lambda *at: (0,) * len(shape), pipeline_mode=pl.Buffered(buffer_count=1)
    )


def params(megabytes):
    return pltpu.CompilerParams(
        dimension_semantics=("arbitrary",), vmem_limit_bytes=megabytes * 1024 * 1024
    )


def cost(flops, bytes_accessed):
    return pl.CostEstimate(
        flops=int(flops), bytes_accessed=int(bytes_accessed), transcendentals=0
    )


def rows_spec(width, rows=BLOCK):
    return pl.BlockSpec((rows, width), lambda t, *_: (t, 0))


def lanes_spec(rows, width):
    return pl.BlockSpec((rows, width), lambda t, *_: (0, t))


def pack(place, w_query, w_key, w_value, w_out):
    width = GRP * GROUP_ALL + D
    return pl.pallas_call(
        pack_kernel,
        grid_spec=pltpu.PrefetchScalarGridSpec(
            num_scalar_prefetch=1,
            grid=(1,),
            in_specs=[whole((ROWS, H * HD)), whole((ROWS, KV * HD)), whole((ROWS, KV * HD)), whole((ROWS, D))],
            out_specs=[whole((ROWS, width)), whole((ROWS // 4, width))],
        ),
        out_shape=[struct((ROWS, width), bf16), struct((ROWS // 4, width), bf16)],
        compiler_params=params(60),
        cost_estimate=cost(1e5, 3e6),
        name="pack",
    )(place, w_query, w_key, w_value, w_out)


def quarters(place, w_gate, w_up, w_down):
    part = ROWS // 4
    rows = 2 * GRP * part + D // 4
    return pl.pallas_call(
        quarters_kernel,
        grid_spec=pltpu.PrefetchScalarGridSpec(
            num_scalar_prefetch=1,
            grid=(1,),
            in_specs=[
                pl.BlockSpec((part, FF), lambda t, p: (p[1], 0)),
                pl.BlockSpec((part, FF), lambda t, p: (p[1], 0)),
                pl.BlockSpec((FF // GRP, D // 4), lambda t, p: (0, p[1])),
            ],
            out_specs=[whole((rows, TILE))] * CHUNKS,
        ),
        out_shape=[struct((rows, TILE), bf16)] * CHUNKS,
        compiler_params=params(60),
        cost_estimate=cost(1e5, 4e6),
        name="quarters",
    )(place, w_gate, w_up, w_down)


def first_norm(tokens, grad, gain):
    count = tokens.shape[0]
    return pl.pallas_call(
        first_kernel,
        grid=(count // BLOCK,),
        in_specs=[rows_spec(D), rows_spec(D), whole((1, D))],
        out_specs=[rows_spec(D), lanes_spec(D, BLOCK), lanes_spec(D, BLOCK)],
        out_shape=[struct((count, D), bf16), struct((D, count), bf16), struct((D, count), bf16)],
        compiler_params=params(60),
        cost_estimate=cost(1e7, 1e7),
        name="first_norm",
    )(tokens, grad, gain)


def attend(part, place, first, pieces, cos, sin, gain, seg_col, seg_row, spread):
    count = first.shape[0]
    steps = GRP // 2
    own, core, far, far_core = pieces
    far_spec = pl.BlockSpec((4, ROWS // 4, GROUP_ALL), lambda t, p: (0, 0, part * steps + t))
    own_spec = pl.BlockSpec((ROWS, GROUP_ALL), lambda t, p: (0, part * steps + t))
    return pl.pallas_call(
        attend_kernel,
        grid_spec=pltpu.PrefetchScalarGridSpec(
            num_scalar_prefetch=1,
            grid=(steps,),
            in_specs=[
                whole((count, D)),
                own_spec,
                own_spec,
                far_spec,
                far_spec,
                whole((count, 128)),
                whole((count, 128)),
                whole((1, GROUP_QK)),
                whole((count, 1)),
                whole((1, count)),
                whole((GROUP_QK, GROUP_QK)),
            ],
            out_specs=[
                lanes_spec(count, GROUP_QK),
                lanes_spec(count, GROUP_QK),
                lanes_spec(count, GROUP_K),
                lanes_spec(count, GROUP_Q),
                lanes_spec(count, GROUP_Q),
                lanes_spec(D, GROUP_ALL),
            ],
            scratch_shapes=[
                pltpu.VMEM((count, count), f32),
                pltpu.VMEM((count, 2 * HD), bf16),
            ],
        ),
        out_shape=[
            struct((count, steps * GROUP_QK), f32),
            struct((count, steps * GROUP_QK), bf16),
            struct((count, steps * GROUP_K), bf16),
            struct((count, steps * GROUP_Q), bf16),
            struct((count, steps * GROUP_Q), f32),
            struct((D, steps * GROUP_ALL), bf16),
        ],
        compiler_params=params(60),
        cost_estimate=cost(1e10, 1.2e7),
        name="attend",
    )(place, first, own, core, far, far_core, cos, sin, gain, seg_col, seg_row, spread)


def middle(place, mixed, tokens, gain, pieces):
    count = tokens.shape[0]
    own, core, far, far_core = pieces
    one = pl.Buffered(buffer_count=1)
    own_spec = pl.BlockSpec((ROWS, D), lambda t, p: (0, 2), pipeline_mode=one)
    far_spec = pl.BlockSpec((4, ROWS // 4, D), lambda t, p: (0, 0, 2), pipeline_mode=one)
    return pl.pallas_call(
        middle_kernel,
        grid_spec=pltpu.PrefetchScalarGridSpec(
            num_scalar_prefetch=1,
            grid=(count // BLOCK,),
            in_specs=[
                rows_spec(D // 2),
                rows_spec(D // 2),
                rows_spec(D),
                whole((1, D)),
                own_spec,
                own_spec,
                far_spec,
                far_spec,
            ],
            out_specs=[rows_spec(D), rows_spec(D), lanes_spec(D, BLOCK), whole((D, D))],
        ),
        out_shape=[
            struct((count, D), f32),
            struct((count, D), bf16),
            struct((D, count), bf16),
            struct((D, D), bf16),
        ],
        compiler_params=params(60),
        cost_estimate=cost(2e9, 1.6e7),
        name="middle",
    )(place, *mixed, tokens, gain, own, core, far, far_core)


def ffn(place, second, second_t, grad, grad_t, weights, i):
    count = second.shape[0]
    (gate, up, core_gate, core_up, down, core_down), (far, far_core) = weights
    tile = [
        pl.BlockSpec((ROWS, TILE), lambda t, p, j=j: (0, (2 * t + j) * CHUNKS + i))
        for j in range(2)
    ]
    one = pl.Buffered(buffer_count=1)
    down_spec = pl.BlockSpec((TILE, D), lambda t, p: (i, 0), pipeline_mode=one)
    gu_spec = pl.BlockSpec((2, 2, 2, ROWS, TILE), lambda t, p: (0, 0, t, 0, 0))
    dn_spec = pl.BlockSpec((1, D, TILE), lambda t, p: (t ^ (p[0] >> 1), 0, 0))
    return pl.pallas_call(
        ffn_kernel,
        grid_spec=pltpu.PrefetchScalarGridSpec(
            num_scalar_prefetch=1,
            grid=(2,),
            in_specs=[
                whole((count, D)),
                whole((D, count)),
                whole((count, D)),
                whole((D, count)),
            ]
            + tile * 4
            + [whole(far.shape)] * 2
            + [down_spec] * 2,
            out_specs=[whole((count, D)), whole((count, D)), gu_spec, gu_spec, dn_spec, dn_spec],
            scratch_shapes=[
                pltpu.VMEM((D, 2 * PAIR), bf16),
                pltpu.VMEM((GRP, TILE, D), bf16),
                pltpu.VMEM((count, PAIR), bf16),
                pltpu.VMEM((count, 2 * PAIR), bf16),
                pltpu.VMEM((count, D), f32),
                pltpu.VMEM((count, D), f32),
            ],
        ),
        out_shape=[
            struct((count, D), bf16),
            struct((count, D), bf16),
            struct((2, 2, GRP, ROWS, TILE), bf16),
            struct((2, 2, GRP, ROWS, TILE), bf16),
            struct((2, D, TILE), bf16),
            struct((2, D, TILE), bf16),
        ],
        compiler_params=params(60),
        cost_estimate=cost(2.9e10, 3.6e7),
        name="ffn",
    )(
        place, second, second_t, grad, grad_t,
        gate, gate, up, up, core_gate, core_gate, core_up, core_up,
        far, far_core, down, core_down,
    )


def after_ffn(residual, grad, gain, outs, second_grads):
    count = residual.shape[0]
    return pl.pallas_call(
        after_kernel,
        grid=(count // BLOCK,),
        in_specs=[rows_spec(D), rows_spec(D), whole((1, D))] + [rows_spec(D)] * 6,
        out_specs=[rows_spec(D), rows_spec(D), rows_spec(D), whole((1, D))],
        out_shape=[
            struct((count, D), bf16),
            struct((count, D), f32),
            struct((count, D), bf16),
            struct((1, D), f32),
        ],
        compiler_params=params(60),
        cost_estimate=cost(2e7, 2.4e7),
        name="after_ffn",
    )(residual, grad, gain, *outs, *second_grads)


def attend_back(
    skip, steps, place, residual_low, w_out, weights, first_t, proj, qk_low, v_low, mixed, lse, cos, sin,
    gain, seg_col, seg_row, spread,
):
    count = residual_low.shape[0]
    held = skip % (GRP // 2)
    step_cols = lambda width, rows=count: pl.BlockSpec((rows, width), lambda t, p: (0, held + t))
    grad_spec = pl.BlockSpec((2, ROWS, GROUP_ALL), lambda t, p: (0, 0, t))
    return pl.pallas_call(
        attend_back_kernel,
        grid_spec=pltpu.PrefetchScalarGridSpec(
            num_scalar_prefetch=1,
            grid=(steps,),
            in_specs=[
                whole((count, D)),
                pl.BlockSpec((ROWS, D), lambda t, p: (skip + t, 0)),
                step_cols(GROUP_ALL, D),
                whole((D, count)),
                step_cols(GROUP_QK),
                step_cols(GROUP_QK),
                step_cols(GROUP_K),
                step_cols(GROUP_Q),
                step_cols(GROUP_Q),
                whole((count, 128)),
                whole((count, 128)),
                whole((1, GROUP_QK)),
                whole((count, 1)),
                whole((1, count)),
                whole((GROUP_QK, GROUP_QK)),
            ],
            out_specs=[whole((count, D)), grad_spec, grad_spec, whole((1, GROUP_QK))],
            scratch_shapes=[
                pltpu.VMEM((count, count), f32),
                pltpu.VMEM((count, GROUP_Q), bf16),
                pltpu.VMEM((count, GROUP_Q), f32),
                pltpu.VMEM((count, GROUP_QK), f32),
                pltpu.VMEM((count, 2 * HD), f32),
                pltpu.VMEM((count, 2 * HD), f32),
                pltpu.VMEM((count, GROUP_ALL), bf16),
                pltpu.VMEM((count, 2 * HD), bf16),
                pltpu.VMEM((count, 2 * HD), bf16),
                pltpu.VMEM((count, D), f32),
            ],
        ),
        out_shape=[
            struct((count, D), bf16),
            struct((2, ROWS, steps * GROUP_ALL), bf16),
            struct((2, ROWS, steps * GROUP_ALL), bf16),
            struct((1, GROUP_QK), f32),
        ],
        compiler_params=params(60),
        cost_estimate=cost(3e10, 2e7),
        name="attend_back",
    )(
        place, residual_low, w_out, weights, first_t, proj, qk_low, v_low, mixed, lse, cos, sin,
        gain, seg_col, seg_row, spread,
    )


def last_norm(tokens, residual_grad, gain, first_grads):
    count = tokens.shape[0]
    return pl.pallas_call(
        last_kernel,
        grid=(count // BLOCK,),
        in_specs=[rows_spec(D), rows_spec(D), whole((1, D))] + [rows_spec(D)] * len(first_grads),
        out_specs=[rows_spec(D), whole((1, D))],
        out_shape=[struct((count, D), bf16), struct((1, D), f32)],
        compiler_params=params(60),
        cost_estimate=cost(2e7, 1.2e7),
        name="last_norm",
    )(tokens, residual_grad, gain, *first_grads)


def finish(i, total, held):
    both_spec = pl.BlockSpec((ROWS, TILE), lambda t: (0, t * CHUNKS + i))
    any_spec = pl.BlockSpec(memory_space=pl.ANY)
    return pl.pallas_call(
        finish_kernel,
        grid=(GRP,),
        in_specs=[
            pl.BlockSpec((ROWS, TILE), lambda t: (t, 0)),
            pl.BlockSpec((ROWS, TILE), lambda t: (GRP + t, 0)),
            pl.BlockSpec((ROWS, TILE), lambda t: (2 * GRP + t, 0)),
        ]
        + [any_spec] * len(held),
        out_specs=[both_spec, both_spec, pl.BlockSpec((TILE, ROWS), lambda t: (i, t))],
        out_shape=[
            struct((ROWS, FF), f32),
            struct((ROWS, FF), f32),
            struct((FF // GRP, D), f32),
        ],
        input_output_aliases={3 + k: k for k in range(len(held))},
        compiler_params=params(60),
        cost_estimate=cost(1e6, 8e6),
        name="finish",
    )(total, total, total, *held)


def split_sums(total):
    return pl.pallas_call(
        split_kernel,
        grid=(GRP,),
        in_specs=[pl.BlockSpec((ROWS, GROUP_ALL), lambda t: (t, 0))],
        out_specs=[
            lanes_spec(ROWS, GROUP_Q),
            lanes_spec(ROWS, GROUP_K),
            lanes_spec(ROWS, GROUP_K),
        ],
        out_shape=[
            struct((ROWS, H * HD), f32),
            struct((ROWS, KV * HD), f32),
            struct((ROWS, KV * HD), f32),
        ],
        compiler_params=params(60),
        cost_estimate=cost(1e6, 4e6),
        name="split_sums",
    )(total)


class Job:
    def __init__(self, stages):
        self.stages, self.done, self.result = stages, False, None
        self.advance(None)

    def advance(self, came):
        try:
            self.wanted = self.stages.send(came)
        except StopIteration as stop:
            self.done, self.wanted, self.result = True, [], stop.value

    def start(self, payloads):
        self.flight = [send(values) for values, (_, send) in zip(payloads, self.wanted)]


def on_device(rep_count):
    core_pairs = [(i, i ^ 1) for i in range(GRP)]
    far_pairs = [(i, i ^ 2) for i in range(GRP)]
    rep_bits = rep_count.bit_length() - 1

    def to_core(values):
        return lax.ppermute(values, "grp", core_pairs)

    def to_far(values):
        return lax.ppermute(values, "grp", far_pairs)

    def by_xor(mask):
        pairs = [(i, i ^ mask) for i in range(rep_count)]
        return lambda values: lax.ppermute(values, "rep", pairs)

    def to_rep(bit):
        return by_xor(1 << bit)

    def ordered(upper, own, other):
        return jnp.concatenate([jnp.where(upper, other, own), jnp.where(upper, own, other)], axis=0)

    def low_sum(terms):
        return sum(term.astype(f32) for term in terms).astype(bf16)

    def half_of(values, upper, axis=0):
        half = values.shape[axis] // 2
        return lax.dynamic_slice_in_dim(values, upper * half, half, axis)

    def core_stages(sent):
        came = yield [(values, to_core) for values in sent]
        return came

    def reduce_stages(kept, came, sent, early=(), stepwise=False):
        rep = lax.axis_index("rep")
        upper_of = lambda bit: (rep >> bit) & 1
        flat = lambda values: values.reshape(-1, values.shape[-1])
        wide = lambda values: values.reshape(2, -1, values.shape[-1])
        join = lambda parts, axis=0: jnp.concatenate(parts, axis=axis) if len(parts) > 1 else parts[0]
        more = yield [(values, to_core) for values in sent]
        came = list(came) + list(more)
        if early:
            terms = [
                join([low_sum([wide(mine), wide(other)]) for mine, other in zip(kept, came)], axis=1)
            ]
            for bit in early:
                upper = upper_of(bit)
                away = low_sum([half_of(term, 1 - upper, 1) for term in terms])
                terms = [half_of(term, upper, 1) for term in terms]
                terms += yield [(away, to_rep(bit))]
            away = low_sum([term[1] for term in terms])
            terms = [term[0] for term in terms]
        else:
            away = join(
                [low_sum([flat(mine[1]), flat(other[1])]) for mine, other in zip(kept, came)]
            )
            terms = [
                join([flat(values[0]) for values in kept]),
                join([flat(values[0]) for values in came]),
            ]
        terms += yield [(away, to_far)]
        for bit in range(rep_bits):
            if bit not in early:
                upper = upper_of(bit)
                away = low_sum([half_of(term, 1 - upper) for term in terms])
                terms = [half_of(term, upper) for term in terms]
                terms += yield [(away, to_rep(bit))]
        total = low_sum(terms)
        if stepwise:
            for bit in reversed(range(rep_bits)):
                (got,) = yield [(total, to_rep(bit))]
                total = ordered(upper_of(bit) == 1, total, got)
            return total
        (total,) = yield [(total, functools.partial(replica_gather, early=early))]
        return total

    def replica_gather(values, early):
        bits = list(early) + [bit for bit in range(rep_bits) if bit not in early]
        whole = lax.all_gather(values, "rep", axis=0, tiled=False)
        size = values.shape
        whole = whole.reshape((2,) * rep_bits + size)
        order = [rep_bits - 1 - bit for bit in bits]
        whole = whole.transpose(order + [rep_bits, rep_bits + 1])
        return whole.reshape(-1, size[-1])

    def small_stages(values):
        for send in [to_core, to_far] + [to_rep(bit) for bit in range(rep_bits)]:
            (got,) = yield [(values, send)]
            values = values + got
        return values

    def beside(run, inputs, starting, ending):
        starting = [job for job in starting if not job.done]
        ending = [job for job in ending if not job.done]
        payloads = [[values for values, _ in job.wanted] for job in starting]
        inputs, payloads = tie(tuple(inputs), payloads)
        for job, group in zip(starting, payloads):
            job.start(group)
        outs = run(*inputs)
        outs, came = tie(outs, [job.flight for job in ending])
        for job, group in zip(ending, came):
            job.advance(group)
        return outs

    def finish_jobs(jobs):
        running, turn = [], 0
        while not all(job.done for job in jobs):
            left = [job for job in jobs if not job.done and job not in [one for one, _ in running]]
            payloads = tie(*[[values for values, _ in job.wanted] for job in left])
            for job, group in zip(left, payloads):
                job.start(group)
            slow = [job for job in left if isinstance(job.wanted[0][1], functools.partial)]
            running += [(job, turn + 3 + 2 * k) for k, job in enumerate(slow)]
            ending = [job for job in left if job not in slow]
            ending += [job for job, due in running if due <= turn or not ending]
            running = [(job, due) for job, due in running if job not in ending]
            for job, group in zip(ending, tie(*[job.flight for job in ending])):
                job.advance(group)
            turn += 1
        return [job.result for job in jobs]

    def body(
        tokens, segments, attn_gain, w_query, w_key, w_value, query_gain, key_gain, w_out, ffn_gain,
        w_gate, w_up, w_down, out_grad,
    ):
        count = tokens.shape[0]
        g = lax.axis_index("grp").astype(jnp.int32)
        low = (lax.axis_index("rep") & 3).astype(jnp.int32)
        place = jnp.stack([g, low])

        to_y, to_z = to_rep(0), to_rep(1)

        def spread_one(quarter):
            return to_y(quarter), to_z(quarter)

        def spread_two(by_y, by_z):
            half = by_y.shape[0] // 2
            return to_z(by_y[:half]), to_y(by_z[half:])

        def far_of(quarter, by_y, by_z, first_half, second_half):
            return jnp.stack(
                [quarter, by_y, by_z, jnp.concatenate([first_half, second_half], axis=0)]
            )

        gains = jnp.concatenate([attn_gain, ffn_gain, query_gain, key_gain, jnp.zeros((96,), bf16)])
        own_attn, q_attn = pack(place, w_query, w_key, w_value, w_out)

        given, q_attn = tie((place, w_gate, w_up, w_down, segments), q_attn)
        x_attn = to_far(q_attn)
        q_ffn = quarters(*given[:4])
        gains = lax.all_gather(gains, "grp", axis=0, tiled=False).astype(f32)
        attn_full = gains[:, :ROWS].reshape(1, D)
        ffn_full = gains[:, ROWS : 2 * ROWS].reshape(1, D)
        query_full = gains[:, 2 * ROWS : 2 * ROWS + 16].reshape(1, HD)
        key_full = gains[:, 2 * ROWS + 16 : 2 * ROWS + 32].reshape(1, HD)
        x_attn, q_ffn, attn_full, segments = tie(x_attn, q_ffn, attn_full, given[4])

        yz_attn, x0 = spread_one(x_attn), to_far(q_ffn[0])
        core_attn = to_core(own_attn)
        first, first_t, grad_t = first_norm(tokens, out_grad, attn_full)
        yz_attn, x0, core_attn, first, segments = tie(yz_attn, x0, core_attn, first, segments)

        two_attn, x1 = spread_two(*yz_attn), to_far(q_ffn[1])
        core_gate, core_up = to_core(w_gate), to_core(w_up)
        places = jnp.arange(count, dtype=jnp.int32)
        seg_col = segments.reshape(count, 1)
        seg_row = segments.reshape(1, count)
        keep = (seg_col == seg_row) & (places[None, :] <= places[:, None])
        position = (jnp.sum(keep.astype(jnp.int32), axis=1) - 1).astype(f32)
        freqs = theta_base ** (-(2.0 * jnp.arange(HD // 2, dtype=f32)) / HD)
        angles = position[:, None] * freqs[None, :]
        cos, sin = jnp.cos(angles), jnp.sin(angles)
        cos = jnp.concatenate([cos, cos, cos, cos], axis=1)
        sin = jnp.concatenate([-sin, sin, -sin, sin], axis=1)
        lane = jnp.arange(GROUP_QK, dtype=jnp.int32) // HD
        spread = jnp.where(lane[:, None] == lane[None, :], 1.0 / HD, 0.0).astype(bf16)
        head_gain = jnp.concatenate([query_full] * (H // GRP) + [key_full] * (KV // GRP), axis=1)
        fold = jnp.where(jnp.arange(GROUP_QK) < GROUP_Q, score_scale * log2_e, 1.0)[None, :]
        two_attn, x1, cos, sin, spread, head_gain, core_gate, core_up = tie(
            two_attn, x1, cos, sin, spread, head_gain, core_gate, core_up
        )

        far_attn = far_of(x_attn, *yz_attn, *two_attn)
        far_core_attn = to_core(far_attn)
        attn_pieces = (own_attn, core_attn, far_attn, far_core_attn)
        inputs = (place, first, attn_pieces, cos, sin, head_gain * fold, seg_col, seg_row, spread)
        inputs, x0, x1, q2 = tie(inputs, x0, x1, q_ffn[2])
        yz0, yz1, x2 = spread_one(x0), spread_one(x1), to_far(q2)
        saved0, inputs, yz0, yz1, x2, w_down = tie(attend(0, *inputs), inputs, yz0, yz1, x2, w_down)
        two0, two1, core_down = spread_two(*yz0), spread_two(*yz1), to_core(w_down)
        saved1, two0, two1, core_down, x2 = tie(attend(1, *inputs), two0, two1, core_down, x2)
        far0 = far_of(x0, *yz0, *two0)
        far1 = far_of(x1, *yz1, *two1)
        mixed = (saved0[3], saved1[3])
        far0, far1, mixed, x2 = tie(far0, far1, mixed, x2)
        far_core0, far_core1, yz2 = to_core(far0), to_core(far1), spread_one(x2)
        middle_out, far_core0, far_core1, yz2 = tie(
            middle(place, mixed, tokens, ffn_full, attn_pieces), far_core0, far_core1, yz2
        )
        residual, second, second_t, out_weights = middle_out
        near = (w_gate, w_up, core_gate, core_up, w_down, core_down)
        fars = [(far0, far_core0), (far1, far_core1), None]

        outs, second_grads, jobs = [], [], []
        for i in range(CHUNKS):
            (out, second_grad, gu_kept, gu_sent, dn_kept, dn_sent) = beside(
                lambda *given, i=i: ffn(*given, i),
                (place, second, second_t, out_grad, grad_t, (near, fars[i])),
                jobs,
                jobs,
            )
            if i == 0:
                out, two2 = tie(out, spread_two(*yz2))
                far2 = far_of(x2, *yz2, *two2)
                second, far2 = tie(second, far2)
            if i == 1:
                out, far_core2 = tie(out, to_core(far2))
                fars[2] = (far2, far_core2)
            outs.append(out)
            second_grads.append(second_grad)
            early = (0,) if i == CHUNKS - 1 else ()
            jobs.append(Job(reduce_stages([gu_kept, dn_kept], [], [gu_sent, dn_sent], early)))

        def after_and_out(*given):
            outputs, residual_grad, residual_low, ffn_gain_grad = after_ffn(*given[:-1])
            wgrad = dot_tn(jnp.concatenate(given[-1], axis=1), residual_low)
            wgrad = wgrad.astype(bf16).reshape(GRP, ROWS, D)
            at = lambda q: lax.dynamic_slice_in_dim(wgrad, g ^ q, 1, 0)
            out_kept = jnp.concatenate([at(0), at(2)], axis=0)
            out_sent = jnp.concatenate([at(1), at(3)], axis=0)
            return outputs, residual_grad, residual_low, ffn_gain_grad, out_kept, out_sent

        outputs, residual_grad, residual_low, ffn_gain_grad, out_kept, out_sent = beside(
            after_and_out,
            (residual, out_grad, ffn_full, outs, second_grads, mixed),
            [jobs[0], jobs[2]],
            [jobs[0], jobs[2]],
        )

        first_grads, head_grads, kepts, cores = [], [], [], []
        to_send = [out_sent]
        for skip, steps in ((0, 2), (2, 1), (3, 1)):
            core_job = Job(core_stages(to_send))
            saved = (saved0, saved1)[skip // 2]
            last = skip == GRP - 1
            first_grad, kept, sent, head_grad = beside(
                lambda *given, skip=skip, steps=steps: attend_back(skip, steps, *given),
                (
                    place, residual_low, out_weights, saved[5], first_t, *saved[:5],
                    cos, sin, head_gain, seg_col, seg_row, spread,
                ),
                jobs + [core_job],
                (jobs[1:] if last else jobs) + [core_job],
            )
            first_grads.append(first_grad)
            head_grads.append(head_grad)
            cores.append(core_job.result[0])
            by_group = [(kept[:, :, :GROUP_ALL], sent[:, :, :GROUP_ALL])]
            if steps == 2:
                by_group.append((kept[:, :, GROUP_ALL:], sent[:, :, GROUP_ALL:]))
            kepts += [pair[0] for pair in by_group]
            to_send = [sent]
        out_came, two_came, one_came = cores
        came = [two_came[:, :, :GROUP_ALL], two_came[:, :, GROUP_ALL:], one_came]
        attn_job = Job(reduce_stages(kepts, came, to_send, stepwise=True))
        out_job = Job(reduce_stages([out_kept], [out_came], [], stepwise=True))
        input_grad, attn_gain_grad = beside(
            last_norm,
            (tokens, residual_grad, attn_full, first_grads),
            jobs[1:] + [attn_job, out_job],
            jobs + [attn_job, out_job],
        )
        jobs += [attn_job, out_job]

        head_grad = sum(head_grads).reshape(GROUP_QK // HD, HD)
        small = jnp.concatenate(
            [
                attn_gain_grad[0],
                ffn_gain_grad[0],
                jnp.sum(head_grad[: GROUP_Q // HD], axis=0),
                jnp.sum(head_grad[GROUP_Q // HD :], axis=0),
            ]
        )
        jobs.append(Job(small_stages(small.reshape(1, -1))))
        sum0, sum1, sum2, attn_sum, out_sum, small = finish_jobs(jobs)
        mine = lambda start, size: lax.dynamic_slice_in_dim(small[0], start + g * size, size, 0)
        held = ()
        for i, total in enumerate((sum0, sum1, sum2)):
            held = finish(i, total, held)
        gate_grad, up_grad, down_grad = held
        query_grad, key_grad, value_grad = split_sums(attn_sum)
        return (
            outputs,
            input_grad,
            mine(0, ROWS),
            query_grad,
            key_grad,
            value_grad,
            mine(2 * D, HD // GRP),
            mine(2 * D + HD, HD // GRP),
            out_sum.astype(f32),
            mine(D, ROWS),
            gate_grad,
            up_grad,
            down_grad,
        )

    return body


def solution(mesh):
    tokens_spec, weight_spec, vector_spec = P(("rep", "grp"), None), P("grp", None), P("grp")
    return jax.shard_map(
        on_device(mesh.shape["rep"]),
        mesh=mesh,
        in_specs=(
            tokens_spec,
            P(("rep", "grp")),
            vector_spec,
            weight_spec,
            weight_spec,
            weight_spec,
            vector_spec,
            vector_spec,
            weight_spec,
            vector_spec,
            weight_spec,
            weight_spec,
            weight_spec,
            tokens_spec,
        ),
        out_specs=(
            tokens_spec,
            tokens_spec,
            vector_spec,
            weight_spec,
            weight_spec,
            weight_spec,
            vector_spec,
            vector_spec,
            weight_spec,
            vector_spec,
            weight_spec,
            weight_spec,
            weight_spec,
        ),
        check_vma=False,
    )
```

```python
import functools

import jax
import jax.numpy as jnp
from jax import lax
from jax.experimental import pallas as pl
from jax.experimental.pallas import tpu as pltpu
from jax.sharding import PartitionSpec as P

D = 1024
H = 16
KV = 8
HD = 64
FF = 4608
SEQ = 1024
GRP = 4
CHUNKS = 3
TILE = FF // GRP // CHUNKS
ROWS = D // GRP
PAIR = 2 * TILE
GROUP_Q = H // GRP * HD
GROUP_K = KV // GRP * HD
GROUP_QK = GROUP_Q + GROUP_K
GROUP_ALL = GROUP_QK + GROUP_K
BLOCK = 256

epsilon = 1e-05
theta_base = 1000000.0
score_scale = HD ** (-0.5)
log2_e = 1.4426950408889634
ln_2 = 0.6931471805599453

f32 = jnp.float32
bf16 = jnp.bfloat16


def dot_nn(left, right):
    return lax.dot_general(left, right, (((1,), (0,)), ((), ())), preferred_element_type=f32)


def dot_nt(left, right):
    return lax.dot_general(left, right, (((1,), (1,)), ((), ())), preferred_element_type=f32)


def dot_tn(left, right):
    return lax.dot_general(left, right, (((0,), (0,)), ((), ())), preferred_element_type=f32)


def rms_scale(values):
    return lax.rsqrt(jnp.mean(values * values, axis=-1, keepdims=True) + epsilon)


def norm_back(grad_unit, unit, inverse):
    return inverse * (grad_unit - unit * jnp.mean(grad_unit * unit, axis=-1, keepdims=True))


def block_of(ref, block, rows):
    return ref.at[pl.ds(pl.multiple_of(block * rows, rows), rows)]


def tie(*values):
    return lax.optimization_barrier(values)


def split_two(values):
    high = values.astype(bf16)
    return high, (values - high.astype(f32)).astype(bf16)


def head_mean(values, spread):
    high, rest = split_two(values)
    return dot_nn(high, spread) + dot_nn(rest, spread)


def swap_halves(values):
    width = values.shape[-1]
    lane = lax.broadcasted_iota(jnp.int32, values.shape, 1)
    ahead = pltpu.roll(values, width - 32, 1)
    behind = pltpu.roll(values, 32, 1)
    return jnp.where((lane & 63) < 32, ahead, behind)


def three_lanes(values):
    high = values.astype(bf16).astype(f32)
    rest = values - high
    mid = rest.astype(bf16).astype(f32)
    lane = lax.broadcasted_iota(jnp.int32, values.shape, 1)
    out = jnp.where(lane == 0, high, jnp.where(lane == 1, mid, jnp.where(lane == 2, rest - mid, 0.0)))
    return out.astype(bf16)


def three_ones(rows):
    lane = lax.broadcasted_iota(jnp.int32, (rows, HD), 1)
    return jnp.where(lane < 3, 1.0, 0.0).astype(bf16)


def fill_mask(mask, seg_col, seg_row):
    count = mask.shape[0]
    for start in range(0, count, BLOCK):
        rows = lax.broadcasted_iota(jnp.int32, (BLOCK, count), 0) + start
        cols = lax.broadcasted_iota(jnp.int32, (BLOCK, count), 1)
        keep = (seg_col[start : start + BLOCK, :] == seg_row[...]) & (cols <= rows)
        mask[start : start + BLOCK, :] = jnp.where(keep, 1.0, 0.0)


def place_rows(place_ref, held, pieces, start=0, stop=None):
    own, core, far, far_core = pieces
    g, low = place_ref[0], place_ref[1]
    rows = held.shape[0] // GRP
    quarter = rows // 4
    block_of(held, g, rows)[...] = own
    block_of(held, g ^ 1, rows)[...] = core
    for q, piece in ((2, far), (3, far_core)):
        for k in range(4):
            block_of(held, (g ^ q) * 4 + (low ^ k), quarter)[...] = piece[k]


def pack_kernel(place_ref, w_query, w_key, w_value, w_out, out, quarter):
    for a in range(GRP):
        start = a * GROUP_ALL
        out[:, start : start + GROUP_Q] = w_query[:, a * GROUP_Q : (a + 1) * GROUP_Q]
        out[:, start + GROUP_Q : start + GROUP_QK] = w_key[:, a * GROUP_K : (a + 1) * GROUP_K]
        out[:, start + GROUP_QK : start + GROUP_ALL] = w_value[:, a * GROUP_K : (a + 1) * GROUP_K]
    out[:, GRP * GROUP_ALL :] = w_out[...]
    quarter[...] = block_of(out, place_ref[1], ROWS // 4)[...]


def quarters_kernel(place_ref, gate, up, down, *outs):
    part = ROWS // 4
    for i, out in enumerate(outs):
        for k, weight in ((0, gate), (1, up)):
            for a in range(GRP):
                first = (a * CHUNKS + i) * TILE
                start = (k * GRP + a) * part
                out[start : start + part, :] = weight[:, first : first + TILE]
        out[2 * GRP * part :, :] = down[i * TILE : (i + 1) * TILE, :].T


def first_kernel(tokens, grad, gain, first, first_t, grad_t):
    inputs = tokens[...].astype(f32)
    low = (inputs * rms_scale(inputs) * gain[...]).astype(bf16)
    first[...] = low
    first_t[...] = low.T
    grad_t[...] = grad[...].T


def attend_kernel(
    place_ref, first, own, core, far, far_core, cos, sin, gain, seg_col, seg_row, spread,
    proj, qk_low, v_low, mixed, lse, weights, mask, ones_v,
):
    count = first.shape[0]
    place_rows(place_ref, weights, (own[...], core[...], far, far_core))

    @pl.when(pl.program_id(0) == 0)
    def _():
        fill_mask(mask, seg_col, seg_row)

    @pl.loop(0, count // BLOCK)
    def _(block):
        rows = pl.ds(pl.multiple_of(block * BLOCK, BLOCK), BLOCK)
        values = dot_nn(first[rows, :], weights[...])
        qk = values[:, :GROUP_QK]
        proj[rows, :] = qk
        inverse = lax.rsqrt(head_mean(qk * qk, spread[...]) + epsilon)
        normed = qk * inverse * gain[...]
        cos_rows = jnp.concatenate([cos[rows, :]] * (GROUP_QK // 128), axis=1)
        sin_rows = jnp.concatenate([sin[rows, :]] * (GROUP_QK // 128), axis=1)
        qk_low[rows, :] = (normed * cos_rows + swap_halves(normed) * sin_rows).astype(bf16)
        v_low[rows, :] = values[:, GROUP_QK:].astype(bf16)

    for j in range(GROUP_K // HD):
        ones_v[:, :HD] = v_low[:, j * HD : (j + 1) * HD]
        ones_v[:, HD:] = jnp.ones((count, HD), bf16)
        keys = qk_low[:, GROUP_Q + j * HD : GROUP_Q + (j + 1) * HD]
        for start in range(0, count, BLOCK):
            stop = start + BLOCK
            pair = jnp.concatenate(
                [
                    qk_low[start:stop, (2 * j + i) * HD : (2 * j + i + 1) * HD]
                    for i in range(2)
                ],
                axis=0,
            )
            scores = dot_nt(pair, keys[:stop])
            keep = mask[start:stop, :stop]
            weights_low = (jnp.exp2(scores) * jnp.concatenate([keep, keep], axis=0)).astype(bf16)
            summed = dot_nn(weights_low, ones_v[:stop, :])
            total = summed[:, HD:]
            part = (summed[:, :HD] / total).astype(bf16)
            log_total = jnp.log2(total)
            for i in range(2):
                lanes = slice((2 * j + i) * HD, (2 * j + i + 1) * HD)
                mixed[start:stop, lanes] = part[i * BLOCK : (i + 1) * BLOCK]
                lse[start:stop, lanes] = log_total[i * BLOCK : (i + 1) * BLOCK]


def attend_back_kernel(
    place_ref, residual_low, w_out, weights, first_t, proj, qk_low, v_low, mixed, lse, cos, sin, gain,
    seg_col, seg_row, spread,
    first_low, kept, sent, gain_grad,
    mask, mixed_grad, delta, grads, key_grad, value_grad, low_grads, key_ext, value_ext, first_grad,
):
    count = residual_low.shape[0]
    step = pl.program_id(0)

    @pl.when(step == 0)
    def _():
        fill_mask(mask, seg_col, seg_row)
        first_grad[...] = jnp.zeros_like(first_grad)
        gain_grad[...] = jnp.zeros_like(gain_grad)

    @pl.loop(0, count // BLOCK)
    def _(block):
        rows = pl.ds(pl.multiple_of(block * BLOCK, BLOCK), BLOCK)
        low = dot_nt(residual_low[rows, :], w_out[...]).astype(bf16)
        mixed_grad[rows, :] = low
        product = low.astype(f32) * mixed[rows, :].astype(f32)
        delta[rows, :] = head_mean(product, spread[:GROUP_Q, :GROUP_Q]) * HD

    for j in range(GROUP_K // HD):
        key_ext[:, :HD] = qk_low[:, GROUP_Q + j * HD : GROUP_Q + (j + 1) * HD]
        key_ext[:, HD:] = three_ones(count)
        value_ext[:, :HD] = v_low[:, j * HD : (j + 1) * HD]
        value_ext[:, HD:] = three_ones(count)
        key_grad[...] = jnp.zeros_like(key_grad)
        value_grad[...] = jnp.zeros_like(value_grad)
        for start in range(0, count, BLOCK):
            stop = start + BLOCK
            query_rows, grad_rows = [], []
            for i in range(2):
                lanes = slice((2 * j + i) * HD, (2 * j + i + 1) * HD)
                query_rows.append(
                    jnp.concatenate(
                        [qk_low[start:stop, lanes], three_lanes(-lse[start:stop, lanes])], axis=1
                    )
                )
                grad_rows.append(
                    jnp.concatenate(
                        [mixed_grad[start:stop, lanes], three_lanes(-delta[start:stop, lanes])],
                        axis=1,
                    )
                )
            query_ext = jnp.concatenate(query_rows, axis=0)
            grad_ext = jnp.concatenate(grad_rows, axis=0)
            keep = mask[start:stop, :stop]
            probs = jnp.exp2(dot_nt(query_ext, key_ext[:stop, :])) * jnp.concatenate(
                [keep, keep], axis=0
            )
            score_grad = (probs * dot_nt(grad_ext, value_ext[:stop, :])).astype(bf16)
            query_grad = dot_nn(score_grad, key_ext[:stop, :]) * score_scale
            for i in range(2):
                lanes = slice((2 * j + i) * HD, (2 * j + i + 1) * HD)
                grads[start:stop, lanes] = query_grad[i * BLOCK : (i + 1) * BLOCK, :HD]
            key_grad[:stop, :] += dot_tn(score_grad, query_ext)
            value_grad[:stop, :] += dot_tn(probs.astype(bf16), grad_ext)
        grads[:, GROUP_Q + j * HD : GROUP_Q + (j + 1) * HD] = key_grad[:, :HD] * ln_2
        low_grads[:, GROUP_QK + j * HD : GROUP_QK + (j + 1) * HD] = value_grad[:, :HD].astype(bf16)

    @pl.loop(0, count // BLOCK)
    def _(block):
        rows = pl.ds(pl.multiple_of(block * BLOCK, BLOCK), BLOCK)
        cos_rows = jnp.concatenate([cos[rows, :]] * (GROUP_QK // 128), axis=1)
        sin_rows = jnp.concatenate([sin[rows, :]] * (GROUP_QK // 128), axis=1)
        turned = grads[rows, :]
        turned = turned * cos_rows - swap_halves(turned) * sin_rows
        qk = proj[rows, :]
        inverse = lax.rsqrt(head_mean(qk * qk, spread[...]) + epsilon)
        unit = qk * inverse
        gain_grad[...] += jnp.sum(turned * unit, axis=0, keepdims=True)
        scaled = turned * gain[...]
        back = inverse * (scaled - unit * head_mean(scaled * unit, spread[...]))
        low_grads[rows, :GROUP_QK] = back.astype(bf16)
        first_grad[rows, :] += dot_nt(low_grads[rows, :], weights[...])

    for x in range(2):
        for c in range(2):
            rows = pl.ds(pl.multiple_of((place_ref[0] ^ (2 * x + c)) * ROWS, ROWS), ROWS)
            part = dot_nn(first_t[rows, :], low_grads[...]).astype(bf16)
            if c == 0:
                kept[x] = part
            else:
                sent[x] = part

    @pl.when(step == pl.num_programs(0) - 1)
    def _():
        first_low[...] = first_grad[...].astype(bf16)


def middle_kernel(
    place_ref, mixed0, mixed1, tokens, gain, own, core, far, far_core, residual, second, second_t, w_out
):
    @pl.when(pl.program_id(0) == 0)
    def _():
        place_rows(place_ref, w_out, (own[...], core[...], far, far_core))

    mixed = jnp.concatenate([mixed0[...], mixed1[...]], axis=1)
    total = tokens[...].astype(f32) + dot_nn(mixed, w_out[...])
    residual[...] = total
    low = (total * rms_scale(total) * gain[...]).astype(bf16)
    second[...] = low
    second_t[...] = low.T


def ffn_kernel(
    place_ref, second, second_t, grad, grad_t,
    gate0, gate1, up0, up1, core_gate0, core_gate1, core_up0, core_up1, far, far_core,
    down, core_down,
    out, second_grad, gu_kept, gu_sent, dn_kept, dn_sent,
    w_both, w_down, inner_low, both_low, out_sum, grad_sum,
):
    step = pl.program_id(0)
    g, low = place_ref[0], place_ref[1]
    odd = (g & 1) == 1
    count = second.shape[0]
    block_rows = min(512, count)
    quarter = ROWS // 4
    for j, (gate, up, core_gate, core_up) in enumerate(
        ((gate0, up0, core_gate0, core_up0), (gate1, up1, core_gate1, core_up1))
    ):
        for k, own, core in ((0, gate, core_gate), (1, up, core_up)):
            lanes = slice(k * PAIR + j * TILE, k * PAIR + (j + 1) * TILE)
            w_both[pl.ds(pl.multiple_of(g * ROWS, ROWS), ROWS), lanes] = own[...]
            w_both[pl.ds(pl.multiple_of((g ^ 1) * ROWS, ROWS), ROWS), lanes] = core[...]
            for q, piece in ((2, far), (3, far_core)):
                for part in range(4):
                    start = ((g ^ q) * 4 + (low ^ part)) * quarter
                    rows = pl.ds(pl.multiple_of((k * GRP + 2 * step + j) * quarter, quarter), quarter)
                    w_both[pl.ds(pl.multiple_of(start, quarter), quarter), lanes] = piece[part, rows, :]

    @pl.when(step == 0)
    def _():
        w_down[g] = down[...]
        w_down[g ^ 1] = core_down[...]
        for q, piece in ((2, far), (3, far_core)):
            for part in range(4):
                lanes = pl.ds(pl.multiple_of((low ^ part) * (D // 4), D // 4), D // 4)
                w_down[g ^ q, :, lanes] = piece[part, 2 * ROWS :, :].T
        out_sum[...] = jnp.zeros_like(out_sum)
        grad_sum[...] = jnp.zeros_like(grad_sum)

    @pl.loop(0, count // block_rows)
    def _(block):
        rows = pl.ds(pl.multiple_of(block * block_rows, block_rows), block_rows)
        both = dot_nn(second[rows, :], w_both[...])
        gate = both[:, :PAIR]
        up = both[:, PAIR:]
        downs = w_down[pl.ds(2 * step, 2)].reshape(PAIR, D)
        inner_grad = dot_nt(grad[rows, :], downs)
        sigmoid = jax.nn.sigmoid(gate)
        silu = gate * sigmoid
        inner = (silu * up).astype(bf16)
        inner_low[rows, :] = inner
        both_low[rows, :PAIR] = (inner_grad * up * (sigmoid + silu * (1.0 - sigmoid))).astype(bf16)
        both_low[rows, PAIR:] = (inner_grad * silu).astype(bf16)
        out_sum[rows, :] += dot_nn(inner, downs)
        grad_sum[rows, :] += dot_nt(both_low[rows, :], w_both[...])

    for x in range(2):
        for c in range(2):
            rows = pl.ds(pl.multiple_of((g ^ (2 * x + c)) * ROWS, ROWS), ROWS)
            part = dot_nn(second_t[rows, :], both_low[...]).astype(bf16)
            target = gu_kept if c == 0 else gu_sent
            for k in range(2):
                for j in range(2):
                    start = k * PAIR + j * TILE
                    target[x, k, j] = part[:, start : start + TILE]

    @pl.loop(0, D // ROWS)
    def _(block):
        rows = pl.ds(pl.multiple_of(block * ROWS, ROWS), ROWS)
        part = dot_nn(grad_t[rows, :], inner_low[...]).astype(bf16)
        dn_kept[0, rows, :] = jnp.where(odd, part[:, TILE:], part[:, :TILE])
        dn_sent[0, rows, :] = jnp.where(odd, part[:, :TILE], part[:, TILE:])

    @pl.when(step == 1)
    def _():
        out[...] = out_sum[...].astype(bf16)
        second_grad[...] = grad_sum[...].astype(bf16)


def after_kernel(
    residual, grad, gain, out0, out1, out2, sg0, sg1, sg2, outputs, residual_grad, residual_low, gain_grad
):
    @pl.when(pl.program_id(0) == 0)
    def _():
        gain_grad[...] = jnp.zeros_like(gain_grad)

    total = residual[...]
    outputs[...] = (
        total + (out0[...].astype(f32) + out1[...].astype(f32) + out2[...].astype(f32))
    ).astype(bf16)
    second_grad = sg0[...].astype(f32) + sg1[...].astype(f32) + sg2[...].astype(f32)
    inverse = rms_scale(total)
    unit = total * inverse
    gain_grad[...] += jnp.sum(second_grad * unit, axis=0, keepdims=True)
    back = grad[...].astype(f32) + norm_back(second_grad * gain[...], unit, inverse)
    residual_grad[...] = back
    residual_low[...] = back.astype(bf16)


def out_kernel(place_ref, mixed0, mixed1, residual_low, kept, sent, mixed):
    for a in range(GRP):
        half = (mixed0, mixed1)[a // 2]
        first = a % 2 * GROUP_Q
        mixed[a] = half[:, first : first + GROUP_Q]
    for x in range(2):
        for c, target in enumerate((kept, sent)):
            part = dot_tn(mixed[place_ref[0] ^ (2 * x + c)], residual_low[...])
            target[x] = part.astype(bf16)


def last_kernel(tokens, residual_grad, gain, *refs):
    *parts, input_grad, gain_grad = refs

    @pl.when(pl.program_id(0) == 0)
    def _():
        gain_grad[...] = jnp.zeros_like(gain_grad)

    inputs = tokens[...].astype(f32)
    first_grad = sum(part[...].astype(f32) for part in parts)
    inverse = rms_scale(inputs)
    unit = inputs * inverse
    gain_grad[...] += jnp.sum(first_grad * unit, axis=0, keepdims=True)
    input_grad[...] = (
        residual_grad[...] + norm_back(first_grad * gain[...], unit, inverse)
    ).astype(bf16)


def finish_kernel(gate, up, down, *refs):
    gate_out, up_out, down_out = refs[-3:]
    gate_out[...] = gate[...].astype(f32)
    up_out[...] = up[...].astype(f32)
    down_out[...] = down[...].astype(f32).T


def split_kernel(block, query, key, value):
    query[...] = block[:, :GROUP_Q].astype(f32)
    key[...] = block[:, GROUP_Q:GROUP_QK].astype(f32)
    value[...] = block[:, GROUP_QK:].astype(f32)


struct = jax.ShapeDtypeStruct


def whole(shape):
    return pl.BlockSpec(
        shape, lambda *at: (0,) * len(shape), pipeline_mode=pl.Buffered(buffer_count=1)
    )


def params(megabytes):
    return pltpu.CompilerParams(
        dimension_semantics=("arbitrary",), vmem_limit_bytes=megabytes * 1024 * 1024
    )


def cost(flops, bytes_accessed):
    return pl.CostEstimate(
        flops=int(flops), bytes_accessed=int(bytes_accessed), transcendentals=0
    )


def rows_spec(width, rows=BLOCK):
    return pl.BlockSpec((rows, width), lambda t, *_: (t, 0))


def lanes_spec(rows, width):
    return pl.BlockSpec((rows, width), lambda t, *_: (0, t))


def pack(place, w_query, w_key, w_value, w_out):
    width = GRP * GROUP_ALL + D
    return pl.pallas_call(
        pack_kernel,
        grid_spec=pltpu.PrefetchScalarGridSpec(
            num_scalar_prefetch=1,
            grid=(1,),
            in_specs=[whole((ROWS, H * HD)), whole((ROWS, KV * HD)), whole((ROWS, KV * HD)), whole((ROWS, D))],
            out_specs=[whole((ROWS, width)), whole((ROWS // 4, width))],
        ),
        out_shape=[struct((ROWS, width), bf16), struct((ROWS // 4, width), bf16)],
        compiler_params=params(60),
        cost_estimate=cost(1e5, 3e6),
        name="pack",
    )(place, w_query, w_key, w_value, w_out)


def quarters(place, w_gate, w_up, w_down):
    part = ROWS // 4
    rows = 2 * GRP * part + D // 4
    return pl.pallas_call(
        quarters_kernel,
        grid_spec=pltpu.PrefetchScalarGridSpec(
            num_scalar_prefetch=1,
            grid=(1,),
            in_specs=[
                pl.BlockSpec((part, FF), lambda t, p: (p[1], 0)),
                pl.BlockSpec((part, FF), lambda t, p: (p[1], 0)),
                pl.BlockSpec((FF // GRP, D // 4), lambda t, p: (0, p[1])),
            ],
            out_specs=[whole((rows, TILE))] * CHUNKS,
        ),
        out_shape=[struct((rows, TILE), bf16)] * CHUNKS,
        compiler_params=params(60),
        cost_estimate=cost(1e5, 4e6),
        name="quarters",
    )(place, w_gate, w_up, w_down)


def first_norm(tokens, grad, gain):
    count = tokens.shape[0]
    return pl.pallas_call(
        first_kernel,
        grid=(count // BLOCK,),
        in_specs=[rows_spec(D), rows_spec(D), whole((1, D))],
        out_specs=[rows_spec(D), lanes_spec(D, BLOCK), lanes_spec(D, BLOCK)],
        out_shape=[struct((count, D), bf16), struct((D, count), bf16), struct((D, count), bf16)],
        compiler_params=params(60),
        cost_estimate=cost(1e7, 1e7),
        name="first_norm",
    )(tokens, grad, gain)


def attend(part, place, first, pieces, cos, sin, gain, seg_col, seg_row, spread):
    count = first.shape[0]
    steps = GRP // 2
    own, core, far, far_core = pieces
    far_spec = pl.BlockSpec((4, ROWS // 4, GROUP_ALL), lambda t, p: (0, 0, part * steps + t))
    own_spec = pl.BlockSpec((ROWS, GROUP_ALL), lambda t, p: (0, part * steps + t))
    return pl.pallas_call(
        attend_kernel,
        grid_spec=pltpu.PrefetchScalarGridSpec(
            num_scalar_prefetch=1,
            grid=(steps,),
            in_specs=[
                whole((count, D)),
                own_spec,
                own_spec,
                far_spec,
                far_spec,
                whole((count, 128)),
                whole((count, 128)),
                whole((1, GROUP_QK)),
                whole((count, 1)),
                whole((1, count)),
                whole((GROUP_QK, GROUP_QK)),
            ],
            out_specs=[
                lanes_spec(count, GROUP_QK),
                lanes_spec(count, GROUP_QK),
                lanes_spec(count, GROUP_K),
                lanes_spec(count, GROUP_Q),
                lanes_spec(count, GROUP_Q),
                lanes_spec(D, GROUP_ALL),
            ],
            scratch_shapes=[
                pltpu.VMEM((count, count), f32),
                pltpu.VMEM((count, 2 * HD), bf16),
            ],
        ),
        out_shape=[
            struct((count, steps * GROUP_QK), f32),
            struct((count, steps * GROUP_QK), bf16),
            struct((count, steps * GROUP_K), bf16),
            struct((count, steps * GROUP_Q), bf16),
            struct((count, steps * GROUP_Q), f32),
            struct((D, steps * GROUP_ALL), bf16),
        ],
        compiler_params=params(60),
        cost_estimate=cost(1e10, 1.2e7),
        name="attend",
    )(place, first, own, core, far, far_core, cos, sin, gain, seg_col, seg_row, spread)


def middle(place, mixed, tokens, gain, pieces):
    count = tokens.shape[0]
    own, core, far, far_core = pieces
    one = pl.Buffered(buffer_count=1)
    own_spec = pl.BlockSpec((ROWS, D), lambda t, p: (0, 2), pipeline_mode=one)
    far_spec = pl.BlockSpec((4, ROWS // 4, D), lambda t, p: (0, 0, 2), pipeline_mode=one)
    return pl.pallas_call(
        middle_kernel,
        grid_spec=pltpu.PrefetchScalarGridSpec(
            num_scalar_prefetch=1,
            grid=(count // BLOCK,),
            in_specs=[
                rows_spec(D // 2),
                rows_spec(D // 2),
                rows_spec(D),
                whole((1, D)),
                own_spec,
                own_spec,
                far_spec,
                far_spec,
            ],
            out_specs=[rows_spec(D), rows_spec(D), lanes_spec(D, BLOCK), whole((D, D))],
        ),
        out_shape=[
            struct((count, D), f32),
            struct((count, D), bf16),
            struct((D, count), bf16),
            struct((D, D), bf16),
        ],
        compiler_params=params(60),
        cost_estimate=cost(2e9, 1.6e7),
        name="middle",
    )(place, *mixed, tokens, gain, own, core, far, far_core)


def ffn(place, second, second_t, grad, grad_t, weights, i):
    count = second.shape[0]
    (gate, up, core_gate, core_up, down, core_down), (far, far_core) = weights
    tile = [
        pl.BlockSpec((ROWS, TILE), lambda t, p, j=j: (0, (2 * t + j) * CHUNKS + i))
        for j in range(2)
    ]
    one = pl.Buffered(buffer_count=1)
    down_spec = pl.BlockSpec((TILE, D), lambda t, p: (i, 0), pipeline_mode=one)
    gu_spec = pl.BlockSpec((2, 2, 2, ROWS, TILE), lambda t, p: (0, 0, t, 0, 0))
    dn_spec = pl.BlockSpec((1, D, TILE), lambda t, p: (t ^ (p[0] >> 1), 0, 0))
    return pl.pallas_call(
        ffn_kernel,
        grid_spec=pltpu.PrefetchScalarGridSpec(
            num_scalar_prefetch=1,
            grid=(2,),
            in_specs=[
                whole((count, D)),
                whole((D, count)),
                whole((count, D)),
                whole((D, count)),
            ]
            + tile * 4
            + [whole(far.shape)] * 2
            + [down_spec] * 2,
            out_specs=[whole((count, D)), whole((count, D)), gu_spec, gu_spec, dn_spec, dn_spec],
            scratch_shapes=[
                pltpu.VMEM((D, 2 * PAIR), bf16),
                pltpu.VMEM((GRP, TILE, D), bf16),
                pltpu.VMEM((count, PAIR), bf16),
                pltpu.VMEM((count, 2 * PAIR), bf16),
                pltpu.VMEM((count, D), f32),
                pltpu.VMEM((count, D), f32),
            ],
        ),
        out_shape=[
            struct((count, D), bf16),
            struct((count, D), bf16),
            struct((2, 2, GRP, ROWS, TILE), bf16),
            struct((2, 2, GRP, ROWS, TILE), bf16),
            struct((2, D, TILE), bf16),
            struct((2, D, TILE), bf16),
        ],
        compiler_params=params(60),
        cost_estimate=cost(2.9e10, 3.6e7),
        name="ffn",
    )(
        place, second, second_t, grad, grad_t,
        gate, gate, up, up, core_gate, core_gate, core_up, core_up,
        far, far_core, down, core_down,
    )


def after_ffn(residual, grad, gain, outs, second_grads):
    count = residual.shape[0]
    return pl.pallas_call(
        after_kernel,
        grid=(count // BLOCK,),
        in_specs=[rows_spec(D), rows_spec(D), whole((1, D))] + [rows_spec(D)] * 6,
        out_specs=[rows_spec(D), rows_spec(D), rows_spec(D), whole((1, D))],
        out_shape=[
            struct((count, D), bf16),
            struct((count, D), f32),
            struct((count, D), bf16),
            struct((1, D), f32),
        ],
        compiler_params=params(60),
        cost_estimate=cost(2e7, 2.4e7),
        name="after_ffn",
    )(residual, grad, gain, *outs, *second_grads)


def attend_back(
    skip, steps, place, residual_low, w_out, weights, first_t, proj, qk_low, v_low, mixed, lse, cos, sin,
    gain, seg_col, seg_row, spread,
):
    count = residual_low.shape[0]
    held = skip % (GRP // 2)
    step_cols = lambda width, rows=count: pl.BlockSpec((rows, width), lambda t, p: (0, held + t))
    grad_spec = pl.BlockSpec((2, ROWS, GROUP_ALL), lambda t, p: (0, 0, t))
    return pl.pallas_call(
        attend_back_kernel,
        grid_spec=pltpu.PrefetchScalarGridSpec(
            num_scalar_prefetch=1,
            grid=(steps,),
            in_specs=[
                whole((count, D)),
                pl.BlockSpec((ROWS, D), lambda t, p: (skip + t, 0)),
                step_cols(GROUP_ALL, D),
                whole((D, count)),
                step_cols(GROUP_QK),
                step_cols(GROUP_QK),
                step_cols(GROUP_K),
                step_cols(GROUP_Q),
                step_cols(GROUP_Q),
                whole((count, 128)),
                whole((count, 128)),
                whole((1, GROUP_QK)),
                whole((count, 1)),
                whole((1, count)),
                whole((GROUP_QK, GROUP_QK)),
            ],
            out_specs=[whole((count, D)), grad_spec, grad_spec, whole((1, GROUP_QK))],
            scratch_shapes=[
                pltpu.VMEM((count, count), f32),
                pltpu.VMEM((count, GROUP_Q), bf16),
                pltpu.VMEM((count, GROUP_Q), f32),
                pltpu.VMEM((count, GROUP_QK), f32),
                pltpu.VMEM((count, 2 * HD), f32),
                pltpu.VMEM((count, 2 * HD), f32),
                pltpu.VMEM((count, GROUP_ALL), bf16),
                pltpu.VMEM((count, 2 * HD), bf16),
                pltpu.VMEM((count, 2 * HD), bf16),
                pltpu.VMEM((count, D), f32),
            ],
        ),
        out_shape=[
            struct((count, D), bf16),
            struct((2, ROWS, steps * GROUP_ALL), bf16),
            struct((2, ROWS, steps * GROUP_ALL), bf16),
            struct((1, GROUP_QK), f32),
        ],
        compiler_params=params(60),
        cost_estimate=cost(3e10, 2e7),
        name="attend_back",
    )(
        place, residual_low, w_out, weights, first_t, proj, qk_low, v_low, mixed, lse, cos, sin,
        gain, seg_col, seg_row, spread,
    )


def out_back(place, mixed0, mixed1, residual_low):
    count = residual_low.shape[0]
    return pl.pallas_call(
        out_kernel,
        grid_spec=pltpu.PrefetchScalarGridSpec(
            num_scalar_prefetch=1,
            grid=(1,),
            in_specs=[whole((count, D // 2)), whole((count, D // 2)), whole((count, D))],
            out_specs=[whole((2, ROWS, D)), whole((2, ROWS, D))],
            scratch_shapes=[pltpu.VMEM((GRP, count, GROUP_Q), bf16)],
        ),
        out_shape=[struct((2, ROWS, D), bf16), struct((2, ROWS, D), bf16)],
        compiler_params=params(60),
        cost_estimate=cost(2e9, 6e6),
        name="out_back",
    )(place, mixed0, mixed1, residual_low)


def last_norm(tokens, residual_grad, gain, first_grads):
    count = tokens.shape[0]
    return pl.pallas_call(
        last_kernel,
        grid=(count // BLOCK,),
        in_specs=[rows_spec(D), rows_spec(D), whole((1, D))] + [rows_spec(D)] * len(first_grads),
        out_specs=[rows_spec(D), whole((1, D))],
        out_shape=[struct((count, D), bf16), struct((1, D), f32)],
        compiler_params=params(60),
        cost_estimate=cost(2e7, 1.2e7),
        name="last_norm",
    )(tokens, residual_grad, gain, *first_grads)


def finish(i, total, held):
    both_spec = pl.BlockSpec((ROWS, TILE), lambda t: (0, t * CHUNKS + i))
    any_spec = pl.BlockSpec(memory_space=pl.ANY)
    return pl.pallas_call(
        finish_kernel,
        grid=(GRP,),
        in_specs=[
            pl.BlockSpec((ROWS, TILE), lambda t: (t, 0)),
            pl.BlockSpec((ROWS, TILE), lambda t: (GRP + t, 0)),
            pl.BlockSpec((ROWS, TILE), lambda t: (2 * GRP + t, 0)),
        ]
        + [any_spec] * len(held),
        out_specs=[both_spec, both_spec, pl.BlockSpec((TILE, ROWS), lambda t: (i, t))],
        out_shape=[
            struct((ROWS, FF), f32),
            struct((ROWS, FF), f32),
            struct((FF // GRP, D), f32),
        ],
        input_output_aliases={3 + k: k for k in range(len(held))},
        compiler_params=params(60),
        cost_estimate=cost(1e6, 8e6),
        name="finish",
    )(total, total, total, *held)


def split_sums(total):
    return pl.pallas_call(
        split_kernel,
        grid=(GRP,),
        in_specs=[pl.BlockSpec((ROWS, GROUP_ALL), lambda t: (t, 0))],
        out_specs=[
            lanes_spec(ROWS, GROUP_Q),
            lanes_spec(ROWS, GROUP_K),
            lanes_spec(ROWS, GROUP_K),
        ],
        out_shape=[
            struct((ROWS, H * HD), f32),
            struct((ROWS, KV * HD), f32),
            struct((ROWS, KV * HD), f32),
        ],
        compiler_params=params(60),
        cost_estimate=cost(1e6, 4e6),
        name="split_sums",
    )(total)


class Job:
    def __init__(self, stages):
        self.stages, self.done, self.result = stages, False, None
        self.advance(None)

    def advance(self, came):
        try:
            self.wanted = self.stages.send(came)
        except StopIteration as stop:
            self.done, self.wanted, self.result = True, [], stop.value

    def start(self, payloads):
        self.flight = [send(values) for values, (_, send) in zip(payloads, self.wanted)]


def on_device(rep_count):
    core_pairs = [(i, i ^ 1) for i in range(GRP)]
    far_pairs = [(i, i ^ 2) for i in range(GRP)]
    rep_bits = rep_count.bit_length() - 1

    def to_core(values):
        return lax.ppermute(values, "grp", core_pairs)

    def to_far(values):
        return lax.ppermute(values, "grp", far_pairs)

    def by_xor(mask):
        pairs = [(i, i ^ mask) for i in range(rep_count)]
        return lambda values: lax.ppermute(values, "rep", pairs)

    def to_rep(bit):
        return by_xor(1 << bit)

    def ordered(upper, own, other):
        return jnp.concatenate([jnp.where(upper, other, own), jnp.where(upper, own, other)], axis=0)

    def low_sum(terms):
        return sum(term.astype(f32) for term in terms).astype(bf16)

    def half_of(values, upper, axis=0):
        half = values.shape[axis] // 2
        return lax.dynamic_slice_in_dim(values, upper * half, half, axis)

    def core_stages(sent):
        came = yield [(values, to_core) for values in sent]
        return came

    def reduce_stages(kept, came, sent, early=(), stepwise=False):
        rep = lax.axis_index("rep")
        upper_of = lambda bit: (rep >> bit) & 1
        flat = lambda values: values.reshape(-1, values.shape[-1])
        wide = lambda values: values.reshape(2, -1, values.shape[-1])
        join = lambda parts, axis=0: jnp.concatenate(parts, axis=axis) if len(parts) > 1 else parts[0]
        more = yield [(values, to_core) for values in sent]
        came = list(came) + list(more)
        if early:
            terms = [
                join([low_sum([wide(mine), wide(other)]) for mine, other in zip(kept, came)], axis=1)
            ]
            for bit in early:
                upper = upper_of(bit)
                away = low_sum([half_of(term, 1 - upper, 1) for term in terms])
                terms = [half_of(term, upper, 1) for term in terms]
                terms += yield [(away, to_rep(bit))]
            away = low_sum([term[1] for term in terms])
            terms = [term[0] for term in terms]
        else:
            away = join(
                [low_sum([flat(mine[1]), flat(other[1])]) for mine, other in zip(kept, came)]
            )
            terms = [
                join([flat(values[0]) for values in kept]),
                join([flat(values[0]) for values in came]),
            ]
        terms += yield [(away, to_far)]
        for bit in range(rep_bits):
            if bit not in early:
                upper = upper_of(bit)
                away = low_sum([half_of(term, 1 - upper) for term in terms])
                terms = [half_of(term, upper) for term in terms]
                terms += yield [(away, to_rep(bit))]
        total = low_sum(terms)
        if stepwise:
            for bit in reversed(range(rep_bits)):
                (got,) = yield [(total, to_rep(bit))]
                total = ordered(upper_of(bit) == 1, total, got)
            return total
        (total,) = yield [(total, functools.partial(replica_gather, early=early))]
        return total

    def replica_gather(values, early):
        bits = list(early) + [bit for bit in range(rep_bits) if bit not in early]
        whole = lax.all_gather(values, "rep", axis=0, tiled=False)
        size = values.shape
        whole = whole.reshape((2,) * rep_bits + size)
        order = [rep_bits - 1 - bit for bit in bits]
        whole = whole.transpose(order + [rep_bits, rep_bits + 1])
        return whole.reshape(-1, size[-1])

    def small_stages(values):
        for send in [to_core, to_far] + [to_rep(bit) for bit in range(rep_bits)]:
            (got,) = yield [(values, send)]
            values = values + got
        return values

    def beside(run, inputs, starting, ending):
        starting = [job for job in starting if not job.done]
        ending = [job for job in ending if not job.done]
        payloads = [[values for values, _ in job.wanted] for job in starting]
        inputs, payloads = tie(tuple(inputs), payloads)
        for job, group in zip(starting, payloads):
            job.start(group)
        outs = run(*inputs)
        outs, came = tie(outs, [job.flight for job in ending])
        for job, group in zip(ending, came):
            job.advance(group)
        return outs

    def finish_jobs(jobs, after, made):
        running, turn = [], 0
        while not all(job.done for job in jobs):
            left = [job for job in jobs if not job.done and job not in [one for one, _ in running]]
            payloads, made = tie([[values for values, _ in job.wanted] for job in left], made)
            for job, group in zip(left, payloads):
                job.start(group)
            slow = [job for job in left if isinstance(job.wanted[0][1], functools.partial)]
            running += [(job, turn + 3 + 2 * k) for k, job in enumerate(slow)]
            ending = [job for job in left if job not in slow]
            ending += [job for job, due in running if due <= turn or not ending]
            running = [(job, due) for job, due in running if job not in ending]
            for job, group in zip(ending, tie(*[job.flight for job in ending])):
                job.advance(group)
                if job.done and job in after:
                    made = after[job](job.result, made)
            turn += 1
        return [job.result for job in jobs], made

    def body(
        tokens, segments, attn_gain, w_query, w_key, w_value, query_gain, key_gain, w_out, ffn_gain,
        w_gate, w_up, w_down, out_grad,
    ):
        count = tokens.shape[0]
        g = lax.axis_index("grp").astype(jnp.int32)
        low = (lax.axis_index("rep") & 3).astype(jnp.int32)
        place = jnp.stack([g, low])

        to_y, to_z = to_rep(0), to_rep(1)

        def spread_one(quarter):
            return to_y(quarter), to_z(quarter)

        def spread_two(by_y, by_z):
            half = by_y.shape[0] // 2
            return to_z(by_y[:half]), to_y(by_z[half:])

        def far_of(quarter, by_y, by_z, first_half, second_half):
            return jnp.stack(
                [quarter, by_y, by_z, jnp.concatenate([first_half, second_half], axis=0)]
            )

        gains = jnp.concatenate([attn_gain, ffn_gain, query_gain, key_gain, jnp.zeros((96,), bf16)])
        own_attn, q_attn = pack(place, w_query, w_key, w_value, w_out)

        given, q_attn = tie((place, w_gate, w_up, w_down, segments), q_attn)
        x_attn = to_far(q_attn)
        q_ffn = quarters(*given[:4])
        gains = lax.all_gather(gains, "grp", axis=0, tiled=False).astype(f32)
        attn_full = gains[:, :ROWS].reshape(1, D)
        ffn_full = gains[:, ROWS : 2 * ROWS].reshape(1, D)
        query_full = gains[:, 2 * ROWS : 2 * ROWS + 16].reshape(1, HD)
        key_full = gains[:, 2 * ROWS + 16 : 2 * ROWS + 32].reshape(1, HD)
        x_attn, q_ffn, attn_full, segments = tie(x_attn, q_ffn, attn_full, given[4])

        yz_attn, x0 = spread_one(x_attn), to_far(q_ffn[0])
        core_attn = to_core(own_attn)
        first, first_t, grad_t = first_norm(tokens, out_grad, attn_full)
        yz_attn, x0, core_attn, first, segments = tie(yz_attn, x0, core_attn, first, segments)

        two_attn, x1 = spread_two(*yz_attn), to_far(q_ffn[1])
        core_gate, core_up = to_core(w_gate), to_core(w_up)
        places = jnp.arange(count, dtype=jnp.int32)
        seg_col = segments.reshape(count, 1)
        seg_row = segments.reshape(1, count)
        keep = (seg_col == seg_row) & (places[None, :] <= places[:, None])
        position = (jnp.sum(keep.astype(jnp.int32), axis=1) - 1).astype(f32)
        freqs = theta_base ** (-(2.0 * jnp.arange(HD // 2, dtype=f32)) / HD)
        angles = position[:, None] * freqs[None, :]
        cos, sin = jnp.cos(angles), jnp.sin(angles)
        cos = jnp.concatenate([cos, cos, cos, cos], axis=1)
        sin = jnp.concatenate([-sin, sin, -sin, sin], axis=1)
        lane = jnp.arange(GROUP_QK, dtype=jnp.int32) // HD
        spread = jnp.where(lane[:, None] == lane[None, :], 1.0 / HD, 0.0).astype(bf16)
        head_gain = jnp.concatenate([query_full] * (H // GRP) + [key_full] * (KV // GRP), axis=1)
        fold = jnp.where(jnp.arange(GROUP_QK) < GROUP_Q, score_scale * log2_e, 1.0)[None, :]
        two_attn, x1, cos, sin, spread, head_gain, core_gate, core_up = tie(
            two_attn, x1, cos, sin, spread, head_gain, core_gate, core_up
        )

        far_attn = far_of(x_attn, *yz_attn, *two_attn)
        far_core_attn = to_core(far_attn)
        attn_pieces = (own_attn, core_attn, far_attn, far_core_attn)
        inputs = (place, first, attn_pieces, cos, sin, head_gain * fold, seg_col, seg_row, spread)
        inputs, x0, x1, q2 = tie(inputs, x0, x1, q_ffn[2])
        yz0, yz1, x2 = spread_one(x0), spread_one(x1), to_far(q2)
        saved0, inputs, yz0, yz1, x2, w_down = tie(attend(0, *inputs), inputs, yz0, yz1, x2, w_down)
        two0, two1, core_down = spread_two(*yz0), spread_two(*yz1), to_core(w_down)
        saved1, two0, two1, core_down, x2 = tie(attend(1, *inputs), two0, two1, core_down, x2)
        far0 = far_of(x0, *yz0, *two0)
        far1 = far_of(x1, *yz1, *two1)
        mixed = (saved0[3], saved1[3])
        far0, far1, mixed, x2 = tie(far0, far1, mixed, x2)
        far_core0, far_core1, yz2 = to_core(far0), to_core(far1), spread_one(x2)
        middle_out, far_core0, far_core1, yz2 = tie(
            middle(place, mixed, tokens, ffn_full, attn_pieces), far_core0, far_core1, yz2
        )
        residual, second, second_t, out_weights = middle_out
        near = (w_gate, w_up, core_gate, core_up, w_down, core_down)
        fars = [(far0, far_core0), (far1, far_core1), None]

        outs, second_grads, jobs = [], [], []
        for i in range(CHUNKS):
            (out, second_grad, gu_kept, gu_sent, dn_kept, dn_sent) = beside(
                lambda *given, i=i: ffn(*given, i),
                (place, second, second_t, out_grad, grad_t, (near, fars[i])),
                jobs,
                jobs,
            )
            if i == 0:
                out, two2 = tie(out, spread_two(*yz2))
                far2 = far_of(x2, *yz2, *two2)
                second, far2 = tie(second, far2)
            if i == 1:
                out, far_core2 = tie(out, to_core(far2))
                fars[2] = (far2, far_core2)
            outs.append(out)
            second_grads.append(second_grad)
            early = (0,) if i == CHUNKS - 1 else ()
            jobs.append(
                Job(reduce_stages([gu_kept, dn_kept], [], [gu_sent, dn_sent], early, early != ()))
            )

        def after_and_out(*given):
            outputs, residual_grad, residual_low, ffn_gain_grad = after_ffn(*given[:-1])
            out_kept, out_sent = out_back(place, *given[-1], residual_low)
            return outputs, residual_grad, residual_low, ffn_gain_grad, out_kept, out_sent

        outputs, residual_grad, residual_low, ffn_gain_grad, out_kept, out_sent = beside(
            after_and_out,
            (residual, out_grad, ffn_full, outs, second_grads, mixed),
            [jobs[0], jobs[2]],
            [jobs[0], jobs[2]],
        )

        first_grads, head_grads, kepts, cores = [], [], [], []
        to_send = [out_sent]
        for skip, steps in ((0, 2), (2, 1), (3, 1)):
            core_job = Job(core_stages(to_send))
            saved = (saved0, saved1)[skip // 2]
            last = skip == GRP - 1
            first_grad, kept, sent, head_grad = beside(
                lambda *given, skip=skip, steps=steps: attend_back(skip, steps, *given),
                (
                    place, residual_low, out_weights, saved[5], first_t, *saved[:5],
                    cos, sin, head_gain, seg_col, seg_row, spread,
                ),
                jobs + [core_job],
                (jobs[1:] if last else jobs) + [core_job],
            )
            first_grads.append(first_grad)
            head_grads.append(head_grad)
            cores.append(core_job.result[0])
            kepts.append(kept)
            to_send = [sent]
            if steps == 1 and not last:
                out_came, two_came = cores
                halves = lambda values, size: [values[:, :, :size], values[:, :, size:]]
                kept_a = halves(kepts[0], GROUP_ALL) + halves(out_kept, D // 2)
                came_a = halves(two_came, GROUP_ALL) + halves(out_came, D // 2)
                jobs.append(Job(reduce_stages(kept_a, came_a, [], stepwise=True)))
                jobs[-1].advance([])
        jobs.append(Job(reduce_stages(kepts[1:], cores[2:], to_send, stepwise=True)))
        input_grad, attn_gain_grad = beside(
            last_norm, (tokens, residual_grad, attn_full, first_grads), jobs[1:], jobs
        )

        head_grad = sum(head_grads).reshape(GROUP_QK // HD, HD)
        small = jnp.concatenate(
            [
                attn_gain_grad[0],
                ffn_gain_grad[0],
                jnp.sum(head_grad[: GROUP_Q // HD], axis=0),
                jnp.sum(head_grad[GROUP_Q // HD :], axis=0),
            ]
        )
        jobs.append(Job(small_stages(small.reshape(1, -1))))
        after = {
            job: lambda total, held, i=i: finish(i, total, held)
            for i, job in enumerate(jobs[:CHUNKS])
        }
        held = after[jobs[0]](jobs[0].result, ()) if jobs[0].done else ()
        results, (gate_grad, up_grad, down_grad) = finish_jobs(jobs, after, held)
        sums_a, sums_b, small = results[CHUNKS:]
        out_sum = jnp.concatenate([sums_a[2 * ROWS : 3 * ROWS], sums_a[3 * ROWS :]], axis=1)
        attn_sum = jnp.concatenate([sums_a[: 2 * ROWS], sums_b], axis=0)
        mine = lambda start, size: lax.dynamic_slice_in_dim(small[0], start + g * size, size, 0)
        query_grad, key_grad, value_grad = split_sums(attn_sum)
        return (
            outputs,
            input_grad,
            mine(0, ROWS),
            query_grad,
            key_grad,
            value_grad,
            mine(2 * D, HD // GRP),
            mine(2 * D + HD, HD // GRP),
            out_sum.astype(f32),
            mine(D, ROWS),
            gate_grad,
            up_grad,
            down_grad,
        )

    return body


def solution(mesh):
    tokens_spec, weight_spec, vector_spec = P(("rep", "grp"), None), P("grp", None), P("grp")
    return jax.shard_map(
        on_device(mesh.shape["rep"]),
        mesh=mesh,
        in_specs=(
            tokens_spec,
            P(("rep", "grp")),
            vector_spec,
            weight_spec,
            weight_spec,
            weight_spec,
            vector_spec,
            vector_spec,
            weight_spec,
            vector_spec,
            weight_spec,
            weight_spec,
            weight_spec,
            tokens_spec,
        ),
        out_specs=(
            tokens_spec,
            tokens_spec,
            vector_spec,
            weight_spec,
            weight_spec,
            weight_spec,
            vector_spec,
            vector_spec,
            weight_spec,
            vector_spec,
            weight_spec,
            weight_spec,
            weight_spec,
        ),
        check_vma=False,
    )
```
